128 devices in a mesh: dp: 16 (over z, x_lo, core), graph: 8 (over y, x_hi).
Axes of the slice: x: 4 (x_hi: 2, x_lo: 2; x = x_hi * 2 + x_lo), y: 4, z: 4, core: 2. Of those that a mesh axis runs over, the one named last changes fastest.
Arguments:
- edge_feats: bfloat16 [131072, 512], P(('dp', 'graph')), may hold values from -24 to 24
- cotangent: bfloat16 [131072, 512], P(('dp', 'graph')), may hold values from -6 to 6
- angle_basis: bfloat16 [16, 1048576], P(None, ('dp', 'graph')), may hold values from -6 to 6
- source_edge: int32 [1048576], P(('dp', 'graph')), may hold values from 0 to 8191
- target_edge: int32 [1048576], P(('dp', 'graph')), may hold values from 0 to 1023
- pair_weight: bfloat16 [512, 512], P('dp'), may hold values from -0.25 to 0.25
- down_weight: bfloat16 [512, 64], P('dp'), may hold values from -0.25 to 0.25
- basis_weight: bfloat16 [16, 64], P('dp'), may hold values from -1.5 to 1.5
- up_weight: bfloat16 [64, 512], P('dp'), may hold values from -0.75 to 0.75
- res_first: bfloat16 [512, 512], P('dp'), may hold values from -0.25 to 0.25
- res_second: bfloat16 [512, 512], P('dp'), may hold values from -0.25 to 0.25
Outputs:
- edge_grad: bfloat16 [131072, 512], P(('dp', 'graph'))
- pair_grad: float32 [512, 512], P('dp')
- down_grad: float32 [512, 64], P('dp')
- basis_grad: float32 [16, 64], P('dp')
- up_grad: float32 [64, 512], P('dp')
- first_grad: float32 [512, 512], P('dp')
- second_grad: float32 [512, 512], P('dp')
The draws below stay inside these ranges and needn't reach their ends.
Inputs may be any that keep to these rules, and one draw needn't show every extreme that they name: source_edge[t] may name any edge of the 8 devices of the triplet's group. target_edge[t] names an edge of the triplet's own device.
All inputs are finite; a program needn't handle non-finite values.
Results may differ from the reference program's by a relative error of at most 0.013.
Values may be sent and summed in bfloat16 or wider, within the bound.
No kernel may reach another device: no remote copies, remote signals or barrier semaphores. Data moves between devices by JAX's collectives and lax.ppermute only.
A program may use at most 64 MiB of HBM per device.

```python
import math
import jax
import jax.numpy as jnp
from jax import lax

D = 512
DT = 64
NCBF = 16
E_DEV = 1024
T_DEV = 8192
E_GRP = 8192
T_GRP = 65536
EDGES = 131072
TRIPS = 1048576
N_DP = 16


def set_ends(entries, key, smallest, high):
    shape = entries.shape
    index_at = [jax.random.randint(jax.random.fold_in(key, axis), (), 0, shape[axis]) for axis in range(len(shape))]
    entries = entries.at[tuple(index_at)].set(smallest)
    longest = shape.index(max(shape))
    index_at[longest] = (index_at[longest] + 1) % shape[longest]
    return entries.at[tuple(index_at)].set(high)


def spiked(drawn, stream_key, source, target, blocks, factor):
    owner, partner = [(jnp.arange(drawn.shape[dim]) // (drawn.shape[dim] // blocks)).reshape([-1 if axis == dim else 1 for axis in range(drawn.ndim)]) for dim in (source, target)]
    chosen = jax.random.permutation(stream_key, blocks)[partner]
    strong = (owner == chosen) | (owner == (partner + blocks // 2) % blocks)
    return jnp.where(strong, factor * drawn, drawn)


def block_scale(rng, extent, shards, least, high):
    def one(dim, blocks):
        draws = jax.random.uniform(jax.random.fold_in(jax.random.fold_in(rng, 6), dim), (blocks,), jnp.float32, least / len(shards), high / len(shards))
        return jnp.repeat(jnp.exp(draws), extent[dim] // blocks).reshape((-1,) + (1,) * (len(extent) - dim - 1))

    loudness = one(*shards[0])
    for cut in shards[1:]:
        loudness = loudness * one(*cut)
    return loudness


def noise(stream_key, shape, deviation, most, shards=(), held_as=jnp.bfloat16):
    array = jax.random.normal(stream_key, shape, jnp.float32) * deviation
    if len(shards) > 0:
        array = block_scale(stream_key, shape, shards, -0.22, 0.18) * array
    return jnp.clip(array, min=-most, max=most).astype(held_as)


def noise_with(rng, dims, deviation, limit, shards, heavy, kind=jnp.bfloat16):
    result = deviation * jax.random.normal(rng, dims, jnp.float32)
    if shards:
        result = result * block_scale(rng, dims, shards, -0.22, 0.18)
    return jnp.clip(spiked(result, jax.random.fold_in(rng, 3), *heavy), -limit, limit).astype(kind)


def setup_inputs(seed: int = 0) -> dict:
    streams_of = jax.random.split(jax.random.key(seed), 12)
    edge_feats = noise_with(streams_of[0], (EDGES, D), 1.0, 24.0, ((0, 128),), (0, 1, 128, 5.5))
    cotangent = noise(streams_of[1], (EDGES, D), 1.0, 6.0, ((0, 128),))
    angle_basis = noise(streams_of[2], (NCBF, TRIPS), 1.0, 6.0, ((1, 128),))
    source_edge = set_ends(jax.random.randint(streams_of[3], (TRIPS,), 0, E_GRP), jax.random.fold_in(streams_of[3], 1), 0, E_GRP - 1).astype(jnp.int32)
    target_edge = set_ends(jax.random.randint(streams_of[4], (TRIPS,), 0, E_DEV), jax.random.fold_in(streams_of[4], 1), 0, E_DEV - 1).astype(jnp.int32)
    pair_weight = noise(streams_of[5], (D, D), D ** -0.5, 0.25, ((0, 16),))
    down_weight = noise(streams_of[6], (D, DT), D ** -0.5, 0.25, ((0, 16),))
    basis_weight = noise(streams_of[7], (NCBF, DT), NCBF ** -0.5, 1.5, ((0, 16),))
    up_weight = noise(streams_of[8], (DT, D), DT ** -0.5, 0.75, ((0, 16),))
    res_first = noise(streams_of[9], (D, D), D ** -0.5, 0.25, ((0, 16),))
    res_second = noise(streams_of[10], (D, D), D ** -0.5, 0.25, ((0, 16),))
    return {"edge_feats": edge_feats, "cotangent": cotangent, "angle_basis": angle_basis, "source_edge": source_edge, "target_edge": target_edge, "pair_weight": pair_weight, "down_weight": down_weight, "basis_weight": basis_weight, "up_weight": up_weight, "res_first": res_first, "res_second": res_second}


def silu_slope(value):
    sig = jax.nn.sigmoid(value)
    return sig * (1.0 + value * (1.0 - sig))

def group_pass(feats, cotan, basis, source, target, pair_weight, down_weight, basis_weight, up_weight, res_first, res_second):
    f32 = jnp.float32
    bf16 = jnp.bfloat16
    scale = math.sqrt(0.5)
    offset = jnp.arange(T_GRP, dtype=jnp.int32) // T_DEV * E_DEV
    outgoing = target + offset
    z_one = jnp.dot(feats, pair_weight, preferred_element_type=f32)
    hidden = jax.nn.silu(z_one).astype(bf16)
    down_t = jnp.einsum('ed,dk->ke', hidden.astype(f32), down_weight.astype(f32)).astype(bf16)
    coeff = jnp.einsum('nk,nt->kt', basis_weight.astype(f32), basis.astype(f32))
    down_in = down_t[:, source].astype(f32)
    agg_t = jnp.zeros((DT, E_GRP), f32).at[:, outgoing].add(down_in * coeff).astype(bf16)
    z_two = jnp.einsum('ke,kd->ed', agg_t.astype(f32), up_weight.astype(f32))
    mixed = jax.nn.silu(z_two).astype(bf16)
    z_three = jnp.dot(mixed, res_first, preferred_element_type=f32)
    inner = jax.nn.silu(z_three).astype(bf16)
    z_four = jnp.dot(inner, res_second, preferred_element_type=f32)
    dz_four = (scale * cotan.astype(f32) * silu_slope(z_four)).astype(bf16)
    second_grad = jnp.dot(inner.T, dz_four, preferred_element_type=f32)
    dz_three = (jnp.dot(dz_four, res_second.T, preferred_element_type=f32) * silu_slope(z_three)).astype(bf16)
    first_grad = jnp.dot(mixed.T, dz_three, preferred_element_type=f32)
    dmixed = scale * cotan.astype(f32) + jnp.dot(dz_three, res_first.T, preferred_element_type=f32)
    dz_two = (dmixed * silu_slope(z_two)).astype(bf16)
    up_grad = jnp.einsum('ke,ed->kd', agg_t.astype(f32), dz_two.astype(f32))
    dagg_t = jnp.einsum('kd,ed->ke', up_weight.astype(f32), dz_two.astype(f32))
    dagg_out = dagg_t[:, outgoing]
    dcoeff = (dagg_out * down_in).astype(bf16)
    basis_grad = jnp.einsum('nt,kt->nk', basis.astype(f32), dcoeff.astype(f32))
    ddown_t = jnp.zeros((DT, E_GRP), f32).at[:, source].add(dagg_out * coeff).astype(bf16)
    down_grad = jnp.einsum('ed,ke->dk', hidden.astype(f32), ddown_t.astype(f32))
    dz_one = (jnp.einsum('ke,dk->ed', ddown_t.astype(f32), down_weight.astype(f32)) * silu_slope(z_one)).astype(bf16)
    pair_grad = jnp.dot(feats.T, dz_one, preferred_element_type=f32)
    edge_grad = jnp.dot(dz_one, pair_weight.T, preferred_element_type=f32).astype(bf16)
    return (edge_grad, (pair_grad, down_grad, basis_grad, up_grad, first_grad, second_grad))

def reference(edge_feats, cotangent, angle_basis, source_edge, target_edge, pair_weight, down_weight, basis_weight, up_weight, res_first, res_second):
    feats = edge_feats.reshape(N_DP, E_GRP, D)
    cotans = cotangent.reshape(N_DP, E_GRP, D)
    bases = jnp.transpose(angle_basis.reshape(NCBF, N_DP, T_GRP), (1, 0, 2))
    sources = source_edge.reshape(N_DP, T_GRP)
    targets = target_edge.reshape(N_DP, T_GRP)
    weights = (pair_weight, down_weight, basis_weight, up_weight, res_first, res_second)
    start = tuple((jnp.zeros(w.shape, jnp.float32) for w in weights))

    def step(carry, items):
        grads, parts = group_pass(items[0], items[1], items[2], items[3], items[4], *weights)
        summed = tuple((c + p for c, p in zip(carry, parts)))
        return (summed, grads)
    totals, grads = lax.scan(step, start, (feats, cotans, bases, sources, targets))
    edge_grad = grads.reshape(EDGES, D)
    return (edge_grad, totals[0], totals[1], totals[2], totals[3], totals[4], totals[5])
```

```python
import functools
import math

import jax
import jax.numpy as jnp
from jax import lax
from jax.experimental import pallas as pl
from jax.experimental.pallas import tpu as pltpu
from jax.sharding import PartitionSpec as P

F32 = jnp.float32
BF16 = jnp.bfloat16
SCALE = math.sqrt(0.5)
NT = (((1,), (1,)), ((), ()))
TN = (((0,), (0,)), ((), ()))
LANES = 128
SMALL_ROWS = 16
CHUNK = 256
GROUP = 20
LINES = 16
PIECE = 512
MIB = 1024 * 1024


def dot(a, b, dims=(((1,), (0,)), ((), ()))):
    return lax.dot_general(a, b, dims, preferred_element_type=F32)


def silu_and_slope(value):
    sig = jax.nn.sigmoid(value)
    return value * sig, sig * (1.0 + value * (1.0 - sig))


def iota(shape, dim):
    return lax.broadcasted_iota(jnp.int32, shape, dim)


def one_hot(index_row, rows):
    hit = iota((rows, index_row.shape[1]), 0) == index_row
    return jnp.where(hit, 1.0, 0.0).astype(BF16)


def spread(value, part_row, parts):
    return jnp.concatenate(
        [jnp.where(part_row == part, value, 0.0) for part in range(parts)], axis=0
    ).astype(BF16)


def pick(stack, part_row, parts):
    width = stack.shape[0] // parts
    total = stack[:width]
    for part in range(1, parts):
        total = jnp.where(part_row == part, stack[part * width : (part + 1) * width], total)
    return total


def call(kernel, out_shape, *operands, scratch=(), vmem=32, smem=(), hbm=(), lazy=()):
    fetched = tuple(hbm) + tuple(lazy)

    def body(*refs):
        refs = list(refs)
        sems = refs.pop()
        places = refs[len(refs) - len(fetched) :]
        refs = refs[: len(refs) - len(fetched)]
        copies = []
        for k, (operand, place) in enumerate(zip(fetched, places)):
            copies.append(pltpu.make_async_copy(refs[operand], place, sems.at[k]))
            copies[-1].start()
            refs[operand] = place
        for copy in copies[: len(hbm)]:
            copy.wait()

        def ready():
            for copy in copies[len(hbm) :]:
                copy.wait()

        if lazy:
            kernel(ready, *refs)
        else:
            kernel(*refs)

    def space(k):
        return pltpu.SMEM if k in smem else pltpu.HBM if k in fetched else pltpu.VMEM

    return pl.pallas_call(
        body if fetched else kernel,
        out_shape=out_shape,
        in_specs=[pl.BlockSpec(memory_space=space(k)) for k in range(len(operands))],
        out_specs=jax.tree.map(lambda _: pl.BlockSpec(memory_space=pltpu.VMEM), out_shape),
        scratch_shapes=list(scratch)
        + [pltpu.VMEM(operands[k].shape, operands[k].dtype) for k in fetched]
        + [pltpu.SemaphoreType.DMA((len(fetched),))] * bool(fetched),
        compiler_params=pltpu.CompilerParams(vmem_limit_bytes=vmem * MIB),
    )(*operands)


def order_kernel(peers, e_dev, source_ref, target_ref, basis_ref, rows_ref, sorted_ref, owner_ref, pos, acc):
    lines, lanes = source_ref.shape
    source = source_ref[...]
    peer = source // e_dev
    hits = jnp.concatenate(
        [jnp.where(peer == p, 1.0, 0.0) for p in range(peers)], axis=0
    ).astype(BF16)
    full = peers * lines
    row, col = iota((lanes, lanes), 0), iota((lanes, lanes), 1)
    before = dot(hits, jnp.where(row < col, 1.0, 0.0).astype(BF16))
    count = dot(hits, jnp.ones((lanes, LANES), BF16)).astype(BF16)
    row, col = iota((full, full), 0), iota((full, full), 1)
    same = row // lines == col // lines
    line_start = dot(jnp.where(same & (col < row), 1.0, 0.0).astype(BF16), count)
    in_peer = dot(jnp.where(same, 1.0, 0.0).astype(BF16), count)
    chunks = (in_peer.astype(jnp.int32) + (CHUNK - 1)) // CHUNK
    first_line = (col // lines < row // lines) & (col % lines == 0)
    first_chunk = dot(
        jnp.where(first_line, 1.0, 0.0).astype(BF16), chunks.astype(F32).astype(BF16)
    ).astype(jnp.int32)
    at = iota((1, LANES), 1)
    owner = jnp.zeros((1, LANES), jnp.int32)
    start = (first_chunk * CHUNK).astype(F32) + line_start
    total = jnp.zeros((lines, lanes), F32)
    for p in range(peers):
        block = slice(p * lines, (p + 1) * lines)
        wide = jnp.concatenate([start[block]] * (lanes // LANES), axis=1)
        total = jnp.where(peer == p, wide + before[block], total)
        if p > 0:
            owner += jnp.where(first_chunk[p * lines : p * lines + 1, :] <= at, 1, 0)
    owner_ref[...] = owner
    pos[...] = total.astype(jnp.int32)

    width = LINES * lanes
    pieces = sorted_ref.shape[1] // PIECE
    nb = basis_ref.shape[0]
    extra = 8

    def line(ref, step):
        return jnp.concatenate(
            [ref[pl.ds(step * LINES + k, 1), :] for k in range(LINES)], axis=1
        )

    acc[...] = jnp.zeros_like(acc)

    def place(step, carry):
        here = line(pos, step)
        src = line(source_ref, step) & (e_dev - 1)
        tgt = line(target_ref, step)
        cols = pl.ds(pl.multiple_of(step * width, width), width)
        index = jnp.concatenate(
            [src % CHUNK, src // CHUNK, tgt % CHUNK, tgt // CHUNK]
            + [jnp.zeros((extra - 4, width), jnp.int32)],
            axis=0,
        )
        value = jnp.concatenate([basis_ref[:, cols].astype(F32), index.astype(F32)], axis=0)
        acc[...] += dot(spread(value, here // PIECE, pieces), one_hot(here % PIECE, PIECE), NT)
        return carry

    lax.fori_loop(0, lines // LINES, place, 0)
    for piece in range(pieces):
        cols = slice(piece * PIECE, (piece + 1) * PIECE)
        base = piece * (nb + extra)
        sorted_ref[:, cols] = acc[base : base + nb, :].astype(BF16)
        rows_ref[:, cols] = acc[base + nb : base + nb + extra, :].astype(jnp.int32)


def forward_kernel(
    ready,
    owner_ref,
    core_ref,
    down_ref,
    rows_ref,
    basis_ref,
    w_basis_ref,
    w_up_ref,
    w_first_ref,
    w_second_ref,
    cot_ref,
    early_ref,
    early_other_ref,
    up_grad_ref,
    dagg_ref,
    down_in_ref,
    second_s,
    first_s,
    agg_acc,
    agg_s,
    mixed_s,
    inner_s,
    dz_four_s,
    dz_three_s,
    dz_two_s,
):
    peers, stack_rows, e_hi = down_ref.shape
    slots = rows_ref.shape[1]
    trip = w_up_ref.shape[0]
    parts = stack_rows // trip
    width = GROUP * CHUNK
    agg_acc[...] = jnp.zeros_like(agg_acc)

    def forward(step, carry):
        cols = pl.ds(pl.multiple_of(step * width, width), width)
        found = []
        for k in range(GROUP):
            here = pl.ds(pl.multiple_of(step * width + k * CHUNK, CHUNK), CHUNK)
            owner = owner_ref[0, step * GROUP + k]
            hot = one_hot(rows_ref[0:1, here], e_hi)
            found.append(pick(dot(down_ref[owner], hot), rows_ref[1:2, here], parts))
        down_in = jnp.concatenate(found, axis=1)
        coeff = dot(w_basis_ref[...], basis_ref[:, cols])
        down_in_ref[:, cols] = down_in.astype(BF16)
        hot_e = one_hot(rows_ref[2:3, cols], e_hi)
        placed = spread(down_in * coeff, rows_ref[3:4, cols], parts)
        agg_acc[...] += dot(hot_e, placed, NT)
        return carry

    lax.fori_loop(0, slots // width, forward, 0)

    ready()
    w_up = w_up_ref[...]
    w_first = w_first_ref[...]
    w_second = w_second_ref[...]
    for q in range(parts):
        rows = slice(q * e_hi, (q + 1) * e_hi)
        agg = agg_acc[:, q * trip : (q + 1) * trip].astype(BF16)
        agg_s[rows, :] = agg
        act, slope_two = silu_and_slope(dot(agg, w_up))
        mixed = act.astype(BF16)
        mixed_s[rows, :] = mixed
        act, slope_three = silu_and_slope(dot(mixed, w_first))
        inner = act.astype(BF16)
        inner_s[rows, :] = inner
        slope_four = silu_and_slope(dot(inner, w_second))[1]
        cot = SCALE * cot_ref[rows, :].astype(F32)
        dz_four = (cot * slope_four).astype(BF16)
        dz_four_s[rows, :] = dz_four
        dz_three = (dot(dz_four, w_second, NT) * slope_three).astype(BF16)
        dz_three_s[rows, :] = dz_three
        dz_two = ((cot + dot(dz_three, w_first, NT)) * slope_two).astype(BF16)
        dz_two_s[rows, :] = dz_two
        dagg_ref[q * trip : (q + 1) * trip, :] = dot(w_up, dz_two, NT).astype(BF16)

    second_s[...] = dot(inner_s[...], dz_four_s[...], TN).astype(BF16)
    first_s[...] = dot(mixed_s[...], dz_three_s[...], TN).astype(BF16)
    up_grad_ref[...] = dot(agg_s[...], dz_two_s[...], TN)
    pairs = early_ref.shape[0]
    share = w_first.shape[0] // (2 * pairs)
    core = core_ref[0]
    for pair in range(pairs):
        for ref, side in ((early_ref, core), (early_other_ref, 1 - core)):
            at = pl.ds(pl.multiple_of((2 * pair + side) * share, share), share)
            ref[pair, :share, :] = second_s[at, :]
            ref[pair, share:, :] = first_s[at, :]


def backward_kernel(
    owner_ref, dagg_ref, rows_ref, basis_ref, w_basis_ref, down_in_ref, partial_ref, basis_grad, total
):
    peers, stack_rows, e_hi = partial_ref.shape
    slots = rows_ref.shape[1]
    trip = w_basis_ref.shape[0]
    parts = stack_rows // trip
    width = GROUP * CHUNK
    basis_grad[...] = jnp.zeros_like(basis_grad)
    total[...] = jnp.zeros_like(total)

    def backward(step, carry):
        cols = pl.ds(pl.multiple_of(step * width, width), width)
        hot_e = one_hot(rows_ref[2:3, cols], e_hi)
        dagg_out = pick(dot(dagg_ref[...], hot_e), rows_ref[3:4, cols], parts)
        dcoeff = (dagg_out * down_in_ref[:, cols].astype(F32)).astype(BF16)
        basis_grad[...] += dot(basis_ref[:, cols], dcoeff, NT)
        coeff = dot(w_basis_ref[...], basis_ref[:, cols])
        placed = spread(dagg_out * coeff, rows_ref[1:2, cols], parts)
        hot = one_hot(rows_ref[0:1, cols], e_hi)
        terms = []
        for k in range(GROUP):
            here = slice(k * CHUNK, (k + 1) * CHUNK)
            terms.append(dot(placed[:, here], hot[:, here], NT))
        for k in range(GROUP):
            total[owner_ref[0, step * GROUP + k]] += terms[k]
        return carry

    lax.fori_loop(0, slots // width, backward, 0)
    partial_ref[...] = total[...].astype(BF16)


def order(source, target, basis, peers, e_dev):
    shape = jax.ShapeDtypeStruct
    trips = source.shape[0]
    slots = trips + peers * CHUNK
    nb = basis.shape[0]
    lines = trips // LANES
    return call(
        functools.partial(order_kernel, peers, e_dev),
        (shape((8, slots), jnp.int32), shape((nb, slots), BF16), shape((1, LANES), jnp.int32)),
        source.reshape(lines, LANES),
        target.reshape(lines, LANES),
        basis,
        scratch=[
            pltpu.VMEM((lines, LANES), jnp.int32),
            pltpu.VMEM((slots // PIECE * (nb + 8), PIECE), F32),
        ],
        hbm=(0, 1, 2),
        vmem=60,
    )


def forward(owner, core, down, rows, basis, w_basis_t, w_up, w_first, w_second, cot):
    shape = jax.ShapeDtypeStruct
    vmem = pltpu.VMEM
    edges, width = cot.shape
    trip = w_up.shape[0]
    nb = basis.shape[0]
    slots = rows.shape[1]
    return call(
        forward_kernel,
        (
            shape((nb // 2, 2 * width // nb, width), BF16),
            shape((nb // 2, 2 * width // nb, width), BF16),
            shape((trip, width), F32),
            shape((edges // CHUNK * trip, CHUNK), BF16),
            shape((trip, slots), BF16),
        ),
        owner,
        core,
        down,
        rows,
        basis,
        w_basis_t,
        w_up,
        w_first,
        w_second,
        cot,
        scratch=[
            vmem((width, width), BF16),
            vmem((width, width), BF16),
            vmem((CHUNK, edges // CHUNK * trip), F32),
            vmem((edges, trip), BF16),
        ]
        + [vmem((edges, width), BF16)] * 5,
        smem=(0, 1),
        hbm=(2, 3, 4, 5),
        lazy=(6, 7, 8, 9),
        vmem=60,
    )


def backward(owner, dagg, rows, basis, w_basis_t, down_in, peers):
    shape = jax.ShapeDtypeStruct
    nb = basis.shape[0]
    trip = w_basis_t.shape[0]
    stack = (peers,) + dagg.shape
    return call(
        backward_kernel,
        (shape(stack, BF16), shape((nb, trip), F32)),
        owner,
        dagg,
        rows,
        basis,
        w_basis_t,
        down_in,
        scratch=[pltpu.VMEM(stack, F32)],
        smem=(0,),
        hbm=(2, 3),
        vmem=40,
    )


def pack_kernel(pair_ref, down_ref, basis_ref, up_ref, first_ref, second_ref, out_ref, small):
    small[...] = jnp.zeros_like(small)
    share = pair_ref.shape[0]
    trip = down_ref.shape[1]
    up_rows = up_ref.shape[0]
    small[:up_rows, :] = up_ref[...].astype(F32)
    small[up_rows : up_rows + 1, :trip] = basis_ref[...].astype(F32)
    place_down(small, down_ref[...].astype(F32))
    rest = small[...].astype(BF16)
    for partner in range(out_ref.shape[0]):
        out_ref[partner, :share, :] = pair_ref[...]
        out_ref[partner, share : 2 * share, :] = second_ref[...]
        out_ref[partner, 2 * share : 3 * share, :] = first_ref[...]
        out_ref[partner, 3 * share :, :] = rest


def place_down(small, down):
    for group in range(down.shape[0] // 8):
        small[8:16, group * LANES : group * LANES + down.shape[1]] = down[
            group * 8 : (group + 1) * 8, :
        ]


def take_down(small, rows, trip):
    return [
        small[8:16, group * LANES : group * LANES + trip] for group in range(rows // 8)
    ]


def down_kernel(core_ref, feats_ref, own_ref, other_ref, down_ref, head_ref):
    rows, width = feats_ref.shape
    peers, stack_rows, block = down_ref.shape
    trip = stack_rows * block // rows
    pairs = own_ref.shape[0]
    share = width // (2 * pairs)
    core = core_ref[0]
    for pair in range(pairs):
        for ref, side in ((own_ref, core), (other_ref, 1 - core)):
            at = pl.ds(pl.multiple_of((2 * pair + side) * share, share), share)
            head_ref[at, :width] = ref[pair, :share, :]
            small = ref[pair, 3 * share :, :].astype(F32)
            down = jnp.concatenate(take_down(small, share, LANES), axis=0)
            head_ref[at, width:] = down.astype(BF16)
    w_pair = head_ref[:, :width]
    w_down = head_ref[:, width : width + trip]
    for part in range(rows // block):
        z_one = dot(feats_ref[part * block : (part + 1) * block, :], w_pair)
        hidden = silu_and_slope(z_one)[0].astype(BF16)
        down_t = dot(hidden, w_down).T.astype(BF16)
        for peer in range(peers):
            down_ref[peer, part * trip : (part + 1) * trip, :] = down_t


def hidden_kernel(
    core_ref,
    feats_ref,
    weights_ref,
    own_ref,
    other_ref,
    hidden_ref,
    slope_ref,
    second_ref,
    first_ref,
    up_ref,
    basis_ref,
    up_s,
    basis_s,
):
    rows, width = feats_ref.shape
    pairs = own_ref.shape[0]
    share = width // (2 * pairs)
    up_rows = up_ref.shape[0] // (2 * pairs)
    trip = basis_ref.shape[0]
    core = core_ref[0]
    for pair in range(pairs):
        for ref, side in ((own_ref, core), (other_ref, 1 - core)):
            at = pl.ds(pl.multiple_of((2 * pair + side) * share, share), share)
            second_ref[at, :] = ref[pair, share : 2 * share, :]
            first_ref[at, :] = ref[pair, 2 * share : 3 * share, :]
            small = ref[pair, 3 * share :, :].astype(F32)
            up_s[2 * pair + side] = small[:up_rows]
            basis_s[2 * pair + side] = small[up_rows : up_rows + 1, :LANES]
    up_ref[...] = jnp.concatenate([up_s[k] for k in range(2 * pairs)], axis=0).astype(BF16)
    basis = jnp.concatenate([basis_s[k] for k in range(2 * pairs)], axis=0)
    basis_ref[...] = basis.T[:trip].astype(BF16)
    w_pair = weights_ref[:, :width]
    for first in range(0, rows, CHUNK):
        block = slice(first, first + CHUNK)
        act, slope = silu_and_slope(dot(feats_ref[block, :], w_pair))
        hidden_ref[block, :] = act.astype(BF16)
        slope_ref[block, :] = slope.astype(BF16)


def tail_kernel(
    core_ref,
    parts_ref,
    hidden_ref,
    slope_ref,
    feats_ref,
    weights_ref,
    basis_ref,
    up_ref,
    early_ref,
    early_other_ref,
    dz_ref,
    mine_ref,
    theirs_ref,
    ddown_s,
    pair_s,
    small,
):
    peers = parts_ref.shape[0]
    rows, width = feats_ref.shape
    trip = ddown_s.shape[1]
    summed = parts_ref[0].astype(F32)
    for peer in range(1, peers):
        summed += parts_ref[peer].astype(F32)
    span = summed.shape[1]
    for part in range(rows // span):
        ddown_s[part * span : (part + 1) * span, :] = summed[
            part * trip : (part + 1) * trip, :
        ].T.astype(BF16)
    w_down = weights_ref[:, width : width + trip]
    for first in range(0, rows, 256):
        block = slice(first, first + 256)
        dz_ref[block, :] = (
            dot(ddown_s[block, :], w_down, NT) * slope_ref[block, :].astype(F32)
        ).astype(BF16)
    down = dot(hidden_ref[...], ddown_s[...], TN)
    pair_s[...] = dot(feats_ref[...], dz_ref[...], TN).astype(BF16)
    owners = basis_ref.shape[0]
    share = width // owners
    up_rows = trip // owners
    small[...] = jnp.zeros_like(small)
    for owner in range(owners):
        small[owner, :up_rows, :] = up_ref[owner * up_rows : (owner + 1) * up_rows, :]
        small[owner, up_rows : up_rows + 1, :trip] = basis_ref[owner : owner + 1, :]
        place_down(small.at[owner], down[owner * share : (owner + 1) * share])
    core = core_ref[0]
    for pair in range(owners // 2):
        for ref, side, half in (
            (mine_ref, core, early_ref),
            (theirs_ref, 1 - core, early_other_ref),
        ):
            owner = 2 * pair + side
            at = pl.ds(pl.multiple_of(owner * share, share), share)
            ref[pair, :share, :] = pair_s[at, :]
            ref[pair, share : share + SMALL_ROWS, :] = small[owner].astype(BF16)
            ref[pair, share + SMALL_ROWS :, :] = half[pair]


def edge_kernel(dz_ref, weights_ref, out_ref):
    out_ref[...] = dot(dz_ref[...], weights_ref[:, : dz_ref.shape[1]], NT).astype(BF16)


def chip_sum_kernel(own_ref, other_ref, out_ref):
    for pair in range(own_ref.shape[0]):
        total = own_ref[pair].astype(F32) + other_ref[pair].astype(F32)
        out_ref[pair] = total.astype(BF16)


def owners_sum_kernel(parts_ref, out_ref):
    total = parts_ref[0].astype(F32)
    for owner in range(1, parts_ref.shape[0]):
        total += parts_ref[owner].astype(F32)
    total = total.astype(BF16)
    for peer in range(out_ref.shape[0]):
        out_ref[peer] = total


def peers_sum_kernel(parts_ref, pair_ref, down_ref, basis_ref, up_ref, first_ref, second_ref):
    share = pair_ref.shape[0]
    trip = down_ref.shape[1]
    up_rows = up_ref.shape[0]
    total = parts_ref[0].astype(F32)
    for peer in range(1, parts_ref.shape[0]):
        total += parts_ref[peer].astype(F32)
    pair_ref[...] = total[:share]
    small = total[share : share + SMALL_ROWS]
    second_ref[...] = total[share + SMALL_ROWS : 2 * share + SMALL_ROWS]
    first_ref[...] = total[2 * share + SMALL_ROWS :]
    up_ref[...] = small[:up_rows]
    basis_ref[...] = small[up_rows : up_rows + 1, :trip]
    for group, rows in enumerate(take_down(small, share, trip)):
        down_ref[group * 8 : (group + 1) * 8, :] = rows


def on_device(
    edge_feats,
    cotangent,
    angle_basis,
    source_edge,
    target_edge,
    pair_weight,
    down_weight,
    basis_weight,
    up_weight,
    res_first,
    res_second,
):
    shape = jax.ShapeDtypeStruct
    vmem = pltpu.VMEM
    owners = lax.axis_size("dp")
    peers = lax.axis_size("graph")
    pairs = owners // 2
    rows, width = edge_feats.shape
    share = pair_weight.shape[0]
    trip = down_weight.shape[1]
    up_rows = up_weight.shape[0]
    nb = angle_basis.shape[0]
    core = (lax.axis_index("dp") % 2).reshape(1)
    same_core = [[2 * pair + side for pair in range(pairs)] for side in range(2)]

    def swap(value):
        return lax.ppermute(value, "dp", [(owner, owner ^ 1) for owner in range(owners)])

    shards = (pair_weight, down_weight, basis_weight, up_weight, res_first, res_second)
    own = call(
        pack_kernel,
        shape((pairs, 3 * share + SMALL_ROWS, width), BF16),
        pair_weight,
        down_weight,
        basis_weight,
        up_weight,
        res_first,
        res_second,
        scratch=[vmem((SMALL_ROWS, width), F32)],
        hbm=range(6),
        vmem=60,
    )
    own = lax.all_to_all(own, "dp", 0, 0, axis_index_groups=same_core)
    other = swap(own)
    index, basis, owner = order(source_edge, target_edge, angle_basis, peers, rows)
    down, head = call(
        down_kernel,
        (
            shape((peers, rows // CHUNK * trip, CHUNK), BF16),
            shape((width, width + LANES), BF16),
        ),
        core,
        edge_feats,
        own,
        other,
        smem=(0,),
        vmem=16,
    )
    down = lax.all_to_all(down, "graph", 0, 0)
    hidden, slope, w_second, w_first, w_up, w_basis_t = call(
        hidden_kernel,
        (
            shape((rows, width), BF16),
            shape((rows, width), BF16),
            shape((width, width), BF16),
            shape((width, width), BF16),
            shape((trip, width), BF16),
            shape((trip, nb), BF16),
        ),
        core,
        edge_feats,
        head,
        own,
        other,
        scratch=[vmem((owners, up_rows, width), F32), vmem((owners, 1, LANES), F32)],
        smem=(0,),
        hbm=(1, 2, 3, 4),
        vmem=60,
    )
    early, early_other, up_grad, dagg, down_in = forward(
        owner, core, down, index, basis, w_basis_t, w_up, w_first, w_second, cotangent
    )
    partial, basis_grad = backward(owner, dagg, index, basis, w_basis_t, down_in, peers)
    parts = lax.all_to_all(partial, "graph", 0, 0)
    half = shape((pairs, 3 * share + SMALL_ROWS, width), BF16)
    dz_one, grads, other = call(
        tail_kernel,
        (shape((rows, width), BF16), half, half),
        core,
        parts,
        hidden,
        slope,
        edge_feats,
        head,
        basis_grad,
        up_grad,
        early,
        early_other,
        scratch=[
            vmem((rows, trip), BF16),
            vmem((width, width), BF16),
            vmem((owners, SMALL_ROWS, width), F32),
        ],
        smem=(0,),
        hbm=(2, 3, 4, 5, 8, 9),
        vmem=32,
    )
    other = swap(other)
    edge_grad = call(edge_kernel, shape((rows, width), BF16), dz_one, head, vmem=16)
    other, edge_grad = lax.optimization_barrier((other, edge_grad))
    chip = call(chip_sum_kernel, half, grads, other, vmem=16)
    chip = lax.all_to_all(chip, "dp", 0, 0, axis_index_groups=same_core)
    sums = call(
        owners_sum_kernel,
        shape((peers, 3 * share + SMALL_ROWS, width), BF16),
        chip,
        vmem=16,
    )
    sums = lax.all_to_all(sums, "graph", 0, 0)
    pair, down_grad, basis_grad, up, first, second = call(
        peers_sum_kernel,
        (
            shape((share, width), F32),
            shape((share, trip), F32),
            shape((1, trip), F32),
            shape((up_rows, width), F32),
            shape((share, width), F32),
            shape((share, width), F32),
        ),
        sums,
        vmem=16,
    )
    return edge_grad, pair, down_grad, basis_grad, up, first, second


def solution(mesh):
    split = P(("dp", "graph"), None)
    line = P(("dp", "graph"))
    rows = P("dp", None)
    return jax.shard_map(
        on_device,
        mesh=mesh,
        in_specs=(split, split, P(None, ("dp", "graph")), line, line) + (rows,) * 6,
        out_specs=(split,) + (rows,) * 6,
        check_vma=False,
    )
```

```python
import functools
import math

import jax
import jax.numpy as jnp
from jax import lax
from jax.experimental import pallas as pl
from jax.experimental.pallas import tpu as pltpu
from jax.sharding import PartitionSpec as P

F32 = jnp.float32
BF16 = jnp.bfloat16
SCALE = math.sqrt(0.5)
NT = (((1,), (1,)), ((), ()))
TN = (((0,), (0,)), ((), ()))
LANES = 128
SMALL_ROWS = 16
CHUNK = 256
GROUP = 20
LINES = 16
PIECE = 512
MIB = 1024 * 1024


def dot(a, b, dims=(((1,), (0,)), ((), ()))):
    return lax.dot_general(a, b, dims, preferred_element_type=F32)


def silu_and_slope(value):
    sig = jax.nn.sigmoid(value)
    return value * sig, sig * (1.0 + value * (1.0 - sig))


def iota(shape, dim):
    return lax.broadcasted_iota(jnp.int32, shape, dim)


def one_hot(index_row, rows):
    hit = iota((rows, index_row.shape[1]), 0) == index_row
    return jnp.where(hit, 1.0, 0.0).astype(BF16)


def spread(value, part_row, parts):
    return jnp.concatenate(
        [jnp.where(part_row == part, value, 0.0) for part in range(parts)], axis=0
    ).astype(BF16)


def pick(stack, part_row, parts):
    width = stack.shape[0] // parts
    total = stack[:width]
    for part in range(1, parts):
        total = jnp.where(part_row == part, stack[part * width : (part + 1) * width], total)
    return total


def call(kernel, out_shape, *operands, scratch=(), vmem=32, smem=(), hbm=(), lazy=()):
    fetched = tuple(hbm) + tuple(lazy)

    def body(*refs):
        refs = list(refs)
        sems = refs.pop()
        places = refs[len(refs) - len(fetched) :]
        refs = refs[: len(refs) - len(fetched)]
        copies = []
        for k, (operand, place) in enumerate(zip(fetched, places)):
            copies.append(pltpu.make_async_copy(refs[operand], place, sems.at[k]))
            copies[-1].start()
            refs[operand] = place
        for copy in copies[: len(hbm)]:
            copy.wait()

        def ready():
            for copy in copies[len(hbm) :]:
                copy.wait()

        if lazy:
            kernel(ready, *refs)
        else:
            kernel(*refs)

    def space(k):
        return pltpu.SMEM if k in smem else pltpu.HBM if k in fetched else pltpu.VMEM

    return pl.pallas_call(
        body if fetched else kernel,
        out_shape=out_shape,
        in_specs=[pl.BlockSpec(memory_space=space(k)) for k in range(len(operands))],
        out_specs=jax.tree.map(lambda _: pl.BlockSpec(memory_space=pltpu.VMEM), out_shape),
        scratch_shapes=list(scratch)
        + [pltpu.VMEM(operands[k].shape, operands[k].dtype) for k in fetched]
        + [pltpu.SemaphoreType.DMA((len(fetched),))] * bool(fetched),
        compiler_params=pltpu.CompilerParams(vmem_limit_bytes=vmem * MIB),
    )(*operands)


def order_kernel(peers, e_dev, source_ref, target_ref, basis_ref, rows_ref, sorted_ref, owner_ref, pos, acc):
    lines, lanes = source_ref.shape
    source = source_ref[...]
    peer = source // e_dev
    hits = jnp.concatenate(
        [jnp.where(peer == p, 1.0, 0.0) for p in range(peers)], axis=0
    ).astype(BF16)
    full = peers * lines
    row, col = iota((lanes, lanes), 0), iota((lanes, lanes), 1)
    before = dot(hits, jnp.where(row < col, 1.0, 0.0).astype(BF16))
    count = dot(hits, jnp.ones((lanes, LANES), BF16)).astype(BF16)
    row, col = iota((full, full), 0), iota((full, full), 1)
    same = row // lines == col // lines
    line_start = dot(jnp.where(same & (col < row), 1.0, 0.0).astype(BF16), count)
    in_peer = dot(jnp.where(same, 1.0, 0.0).astype(BF16), count)
    chunks = (in_peer.astype(jnp.int32) + (CHUNK - 1)) // CHUNK
    first_line = (col // lines < row // lines) & (col % lines == 0)
    first_chunk = dot(
        jnp.where(first_line, 1.0, 0.0).astype(BF16), chunks.astype(F32).astype(BF16)
    ).astype(jnp.int32)
    at = iota((1, LANES), 1)
    owner = jnp.zeros((1, LANES), jnp.int32)
    start = (first_chunk * CHUNK).astype(F32) + line_start
    total = jnp.zeros((lines, lanes), F32)
    for p in range(peers):
        block = slice(p * lines, (p + 1) * lines)
        wide = jnp.concatenate([start[block]] * (lanes // LANES), axis=1)
        total = jnp.where(peer == p, wide + before[block], total)
        if p > 0:
            owner += jnp.where(first_chunk[p * lines : p * lines + 1, :] <= at, 1, 0)
    owner_ref[...] = owner
    pos[...] = total.astype(jnp.int32)

    width = LINES * lanes
    pieces = sorted_ref.shape[1] // PIECE
    nb = basis_ref.shape[0]
    extra = 8

    def line(ref, step):
        return jnp.concatenate(
            [ref[pl.ds(step * LINES + k, 1), :] for k in range(LINES)], axis=1
        )

    acc[...] = jnp.zeros_like(acc)

    def place(step, carry):
        here = line(pos, step)
        src = line(source_ref, step) & (e_dev - 1)
        tgt = line(target_ref, step)
        cols = pl.ds(pl.multiple_of(step * width, width), width)
        index = jnp.concatenate(
            [src % CHUNK, src // CHUNK, tgt % CHUNK, tgt // CHUNK]
            + [jnp.zeros((extra - 4, width), jnp.int32)],
            axis=0,
        )
        value = jnp.concatenate([basis_ref[:, cols].astype(F32), index.astype(F32)], axis=0)
        acc[...] += dot(spread(value, here // PIECE, pieces), one_hot(here % PIECE, PIECE), NT)
        return carry

    lax.fori_loop(0, lines // LINES, place, 0)
    for piece in range(pieces):
        cols = slice(piece * PIECE, (piece + 1) * PIECE)
        base = piece * (nb + extra)
        sorted_ref[:, cols] = acc[base : base + nb, :].astype(BF16)
        rows_ref[:, cols] = acc[base + nb : base + nb + extra, :].astype(jnp.int32)


def rows_of(owner, share):
    return pl.ds(pl.multiple_of(owner * share, share), share)


def middle_kernel(
    ready,
    slot_ref,
    core_ref,
    down_ref,
    rows_ref,
    basis_ref,
    own_ref,
    other_ref,
    cot_ref,
    partial_ref,
    early_ref,
    early_other_ref,
    up_grad_ref,
    basis_grad_ref,
    w_first_s,
    w_second_s,
    up_s,
    basis_s,
    agg_acc,
    agg_s,
    mixed_s,
    inner_s,
    dz_four_s,
    dz_three_s,
    dz_two_s,
    dagg_s,
    down_in_s,
    coeff_s,
    total,
):
    peers, stack_rows, e_hi = down_ref.shape
    slots = rows_ref.shape[1]
    pairs = own_ref.shape[0]
    parts = mixed_s.shape[0] // e_hi
    trip = stack_rows // parts
    width = GROUP * CHUNK
    share = w_first_s.shape[0] // (2 * pairs)
    up_rows = up_s.shape[1]
    core = core_ref[0]

    for pair in range(pairs):
        for ref, side in ((own_ref, core), (other_ref, 1 - core)):
            owner = 2 * pair + side
            w_second_s[rows_of(owner, share), :] = ref[pair, share : 2 * share, :]
            w_first_s[rows_of(owner, share), :] = ref[pair, 2 * share : 3 * share, :]
            small = ref[pair, 3 * share :, :].astype(F32)
            up_s[owner] = small[:up_rows]
            basis_s[owner] = small[up_rows : up_rows + 1, :LANES]
    w_up = jnp.concatenate([up_s[k] for k in range(2 * pairs)], axis=0).astype(BF16)
    w_basis = jnp.concatenate([basis_s[k] for k in range(2 * pairs)], axis=0)
    w_basis = w_basis.T[:trip].astype(BF16)
    agg_acc[...] = jnp.zeros_like(agg_acc)

    def forward(step, carry):
        cols = pl.ds(pl.multiple_of(step * width, width), width)
        found = []
        for k in range(GROUP):
            here = pl.ds(pl.multiple_of(step * width + k * CHUNK, CHUNK), CHUNK)
            slot = slot_ref[0, step * GROUP + k]
            hot = one_hot(rows_ref[0:1, here], e_hi)
            found.append(pick(dot(down_ref[slot], hot), rows_ref[1:2, here], parts))
        down_in = jnp.concatenate(found, axis=1)
        coeff = dot(w_basis, basis_ref[:, cols])
        down_in_s[:, cols] = down_in.astype(BF16)
        coeff_s[:, cols] = coeff
        hot_e = one_hot(rows_ref[2:3, cols], e_hi)
        placed = spread(down_in * coeff, rows_ref[3:4, cols], parts)
        agg_acc[...] += dot(hot_e, placed, NT)
        return carry

    lax.fori_loop(0, slots // width, forward, 0)

    ready()
    w_first = w_first_s[...]
    w_second = w_second_s[...]
    for q in range(parts):
        rows = slice(q * e_hi, (q + 1) * e_hi)
        agg_s[rows, :] = agg_acc[:, q * trip : (q + 1) * trip].astype(BF16)
    step = 2 * e_hi
    for start in range(0, mixed_s.shape[0], step):
        rows = slice(start, start + step)
        act, slope_two = silu_and_slope(dot(agg_s[rows, :], w_up))
        mixed = act.astype(BF16)
        mixed_s[rows, :] = mixed
        act, slope_three = silu_and_slope(dot(mixed, w_first))
        inner = act.astype(BF16)
        inner_s[rows, :] = inner
        slope_four = silu_and_slope(dot(inner, w_second))[1]
        cot = SCALE * cot_ref[rows, :].astype(F32)
        dz_four = (cot * slope_four).astype(BF16)
        dz_four_s[rows, :] = dz_four
        dz_three = (dot(dz_four, w_second, NT) * slope_three).astype(BF16)
        dz_three_s[rows, :] = dz_three
        dz_two_s[rows, :] = ((cot + dot(dz_three, w_first, NT)) * slope_two).astype(BF16)
    for q in range(parts):
        rows = slice(q * e_hi, (q + 1) * e_hi)
        dagg_s[q * trip : (q + 1) * trip, :] = dot(w_up, dz_two_s[rows, :], NT).astype(BF16)

    w_second_s[...] = dot(inner_s[...], dz_four_s[...], TN).astype(BF16)
    w_first_s[...] = dot(mixed_s[...], dz_three_s[...], TN).astype(BF16)
    up_grad_ref[...] = dot(agg_s[...], dz_two_s[...], TN)
    for pair in range(pairs):
        for ref, side in ((early_ref, core), (early_other_ref, 1 - core)):
            at = rows_of(2 * pair + side, share)
            ref[pair, :share, :] = w_second_s[at, :]
            ref[pair, share:, :] = w_first_s[at, :]

    basis_grad_ref[...] = jnp.zeros_like(basis_grad_ref)
    total[...] = jnp.zeros_like(total)

    def backward(step, carry):
        cols = pl.ds(pl.multiple_of(step * width, width), width)
        hot_e = one_hot(rows_ref[2:3, cols], e_hi)
        dagg_out = pick(dot(dagg_s[...], hot_e), rows_ref[3:4, cols], parts)
        dcoeff = (dagg_out * down_in_s[:, cols].astype(F32)).astype(BF16)
        basis_grad_ref[...] += dot(basis_ref[:, cols], dcoeff, NT)
        placed = spread(dagg_out * coeff_s[:, cols], rows_ref[1:2, cols], parts)
        hot = one_hot(rows_ref[0:1, cols], e_hi)
        terms = []
        for k in range(GROUP):
            here = slice(k * CHUNK, (k + 1) * CHUNK)
            terms.append(dot(placed[:, here], hot[:, here], NT))
        for k in range(GROUP):
            total[slot_ref[0, step * GROUP + k]] += terms[k]
        return carry

    lax.fori_loop(0, slots // width, backward, 0)
    partial_ref[...] = total[...].astype(BF16)


def order(source, target, basis, peers, e_dev):
    shape = jax.ShapeDtypeStruct
    trips = source.shape[0]
    slots = trips + peers * CHUNK
    nb = basis.shape[0]
    lines = trips // LANES
    return call(
        functools.partial(order_kernel, peers, e_dev),
        (shape((8, slots), jnp.int32), shape((nb, slots), BF16), shape((1, LANES), jnp.int32)),
        source.reshape(lines, LANES),
        target.reshape(lines, LANES),
        basis,
        scratch=[
            pltpu.VMEM((lines, LANES), jnp.int32),
            pltpu.VMEM((slots // PIECE * (nb + 8), PIECE), F32),
        ],
        hbm=(0, 1, 2),
        vmem=60,
    )


def middle(slot, core, down, rows, basis, own, other, cot):
    shape = jax.ShapeDtypeStruct
    vmem = pltpu.VMEM
    edges, width = cot.shape
    peers, stack_rows, e_hi = down.shape
    trip = stack_rows * e_hi // edges
    nb = basis.shape[0]
    slots = rows.shape[1]
    half = shape((nb // 2, 2 * width // nb, width), BF16)
    return call(
        middle_kernel,
        (shape(down.shape, BF16), half, half, shape((trip, width), F32), shape((nb, trip), F32)),
        slot,
        core,
        down,
        rows,
        basis,
        own,
        other,
        cot,
        scratch=[
            vmem((width, width), BF16),
            vmem((width, width), BF16),
            vmem((nb, trip // nb, width), F32),
            vmem((nb, 1, LANES), F32),
            vmem((e_hi, stack_rows), F32),
            vmem((edges, trip), BF16),
        ]
        + [vmem((edges, width), BF16)] * 5
        + [
            vmem((stack_rows, e_hi), BF16),
            vmem((trip, slots), BF16),
            vmem((trip, slots), F32),
            vmem(down.shape, F32),
        ],
        smem=(0, 1),
        hbm=(2, 3, 4, 5, 6),
        lazy=(7,),
        vmem=60,
    )


def pack_kernel(pair_ref, down_ref, basis_ref, up_ref, first_ref, second_ref, out_ref, small):
    small[...] = jnp.zeros_like(small)
    share = pair_ref.shape[0]
    trip = down_ref.shape[1]
    up_rows = up_ref.shape[0]
    small[:up_rows, :] = up_ref[...].astype(F32)
    small[up_rows : up_rows + 1, :trip] = basis_ref[...].astype(F32)
    place_down(small, down_ref[...].astype(F32))
    rest = small[...].astype(BF16)
    for partner in range(out_ref.shape[0]):
        out_ref[partner, :share, :] = pair_ref[...]
        out_ref[partner, share : 2 * share, :] = second_ref[...]
        out_ref[partner, 2 * share : 3 * share, :] = first_ref[...]
        out_ref[partner, 3 * share :, :] = rest


def place_down(small, down):
    for group in range(down.shape[0] // 8):
        small[8:16, group * LANES : group * LANES + down.shape[1]] = down[
            group * 8 : (group + 1) * 8, :
        ]


def take_down(small, rows, trip):
    return [
        small[8:16, group * LANES : group * LANES + trip] for group in range(rows // 8)
    ]


def down_kernel(core_ref, feats_ref, own_ref, other_ref, down_ref, head_ref):
    rows, width = feats_ref.shape
    peers, stack_rows, block = down_ref.shape
    trip = stack_rows * block // rows
    pairs = own_ref.shape[0]
    share = width // (2 * pairs)
    core = core_ref[0]
    for pair in range(pairs):
        for ref, side in ((own_ref, core), (other_ref, 1 - core)):
            at = pl.ds(pl.multiple_of((2 * pair + side) * share, share), share)
            head_ref[at, :width] = ref[pair, :share, :]
            small = ref[pair, 3 * share :, :].astype(F32)
            down = jnp.concatenate(take_down(small, share, LANES), axis=0)
            head_ref[at, width:] = down.astype(BF16)
    w_pair = head_ref[:, :width]
    w_down = head_ref[:, width : width + trip]
    for part in range(rows // block):
        z_one = dot(feats_ref[part * block : (part + 1) * block, :], w_pair)
        hidden = silu_and_slope(z_one)[0].astype(BF16)
        down_t = dot(hidden, w_down).T.astype(BF16)
        for peer in range(peers):
            down_ref[peer, part * trip : (part + 1) * trip, :] = down_t


def tail_kernel(
    core_ref,
    parts_ref,
    feats_ref,
    weights_ref,
    basis_ref,
    up_ref,
    early_ref,
    early_other_ref,
    dz_ref,
    mine_ref,
    theirs_ref,
    hidden_s,
    ddown_s,
    pair_s,
    small,
):
    peers = parts_ref.shape[0]
    rows, width = feats_ref.shape
    trip = ddown_s.shape[1]
    summed = parts_ref[0].astype(F32)
    for peer in range(1, peers):
        summed += parts_ref[peer].astype(F32)
    span = summed.shape[1]
    for part in range(rows // span):
        ddown_s[part * span : (part + 1) * span, :] = summed[
            part * trip : (part + 1) * trip, :
        ].T.astype(BF16)
    w_down = weights_ref[:, width : width + trip]
    w_pair = weights_ref[:, :width]
    for first in range(0, rows, 512):
        block = slice(first, first + 512)
        act, slope = silu_and_slope(dot(feats_ref[block, :], w_pair))
        hidden_s[block, :] = act.astype(BF16)
        dz_ref[block, :] = (dot(ddown_s[block, :], w_down, NT) * slope).astype(BF16)
    down = dot(hidden_s[...], ddown_s[...], TN)
    pair_s[...] = dot(feats_ref[...], dz_ref[...], TN).astype(BF16)
    owners = basis_ref.shape[0]
    share = width // owners
    up_rows = trip // owners
    small[...] = jnp.zeros_like(small)
    for owner in range(owners):
        small[owner, :up_rows, :] = up_ref[owner * up_rows : (owner + 1) * up_rows, :]
        small[owner, up_rows : up_rows + 1, :trip] = basis_ref[owner : owner + 1, :]
        place_down(small.at[owner], down[owner * share : (owner + 1) * share])
    core = core_ref[0]
    for pair in range(owners // 2):
        for ref, side, half in (
            (mine_ref, core, early_ref),
            (theirs_ref, 1 - core, early_other_ref),
        ):
            owner = 2 * pair + side
            ref[pair, :share, :] = pair_s[rows_of(owner, share), :]
            ref[pair, share : share + SMALL_ROWS, :] = small[owner].astype(BF16)
            ref[pair, share + SMALL_ROWS :, :] = half[pair]


def edge_kernel(dz_ref, weights_ref, out_ref):
    out_ref[...] = dot(dz_ref[...], weights_ref[:, : dz_ref.shape[1]], NT).astype(BF16)


def chip_sum_kernel(own_ref, other_ref, out_ref):
    for pair in range(own_ref.shape[0]):
        total = own_ref[pair].astype(F32) + other_ref[pair].astype(F32)
        out_ref[pair] = total.astype(BF16)


def owners_sum_kernel(parts_ref, out_ref):
    total = parts_ref[0].astype(F32)
    for owner in range(1, parts_ref.shape[0]):
        total += parts_ref[owner].astype(F32)
    total = total.astype(BF16)
    for peer in range(out_ref.shape[0]):
        out_ref[peer] = total


def peers_sum_kernel(parts_ref, pair_ref, down_ref, basis_ref, up_ref, first_ref, second_ref):
    share = pair_ref.shape[0]
    trip = down_ref.shape[1]
    up_rows = up_ref.shape[0]
    total = parts_ref[0].astype(F32)
    for peer in range(1, parts_ref.shape[0]):
        total += parts_ref[peer].astype(F32)
    pair_ref[...] = total[:share]
    small = total[share : share + SMALL_ROWS]
    second_ref[...] = total[share + SMALL_ROWS : 2 * share + SMALL_ROWS]
    first_ref[...] = total[2 * share + SMALL_ROWS :]
    up_ref[...] = small[:up_rows]
    basis_ref[...] = small[up_rows : up_rows + 1, :trip]
    for group, rows in enumerate(take_down(small, share, trip)):
        down_ref[group * 8 : (group + 1) * 8, :] = rows


def on_device(
    edge_feats,
    cotangent,
    angle_basis,
    source_edge,
    target_edge,
    pair_weight,
    down_weight,
    basis_weight,
    up_weight,
    res_first,
    res_second,
):
    shape = jax.ShapeDtypeStruct
    vmem = pltpu.VMEM
    owners = lax.axis_size("dp")
    peers = lax.axis_size("graph")
    pairs = owners // 2
    rows, width = edge_feats.shape
    share = pair_weight.shape[0]
    trip = down_weight.shape[1]
    up_rows = up_weight.shape[0]
    nb = angle_basis.shape[0]
    core = (lax.axis_index("dp") % 2).reshape(1)
    same_core = [[2 * pair + side for pair in range(pairs)] for side in range(2)]

    def swap(value):
        return lax.ppermute(value, "dp", [(owner, owner ^ 1) for owner in range(owners)])

    shards = (pair_weight, down_weight, basis_weight, up_weight, res_first, res_second)
    own = call(
        pack_kernel,
        shape((pairs, 3 * share + SMALL_ROWS, width), BF16),
        pair_weight,
        down_weight,
        basis_weight,
        up_weight,
        res_first,
        res_second,
        scratch=[vmem((SMALL_ROWS, width), F32)],
        hbm=range(6),
        vmem=60,
    )
    own, source_edge = lax.optimization_barrier((own, source_edge))
    own = lax.all_to_all(own, "dp", 0, 0, axis_index_groups=same_core)
    index, basis, slot = order(source_edge, target_edge, angle_basis, peers, rows)
    own, index = lax.optimization_barrier((own, index))
    other = swap(own)
    down, head = call(
        down_kernel,
        (
            shape((peers, rows // CHUNK * trip, CHUNK), BF16),
            shape((width, width + LANES), BF16),
        ),
        core,
        edge_feats,
        own,
        other,
        smem=(0,),
        vmem=16,
    )
    down = lax.all_to_all(down, "graph", 0, 0)
    partial, early, early_other, up_grad, basis_grad = middle(
        slot, core, down, index, basis, own, other, cotangent
    )
    parts = lax.all_to_all(partial, "graph", 0, 0)
    half = shape((pairs, 3 * share + SMALL_ROWS, width), BF16)
    dz_one, grads, other = call(
        tail_kernel,
        (shape((rows, width), BF16), half, half),
        core,
        parts,
        edge_feats,
        head,
        basis_grad,
        up_grad,
        early,
        early_other,
        scratch=[
            vmem((rows, width), BF16),
            vmem((rows, trip), BF16),
            vmem((width, width), BF16),
            vmem((owners, SMALL_ROWS, width), F32),
        ],
        smem=(0,),
        vmem=32,
    )
    other = swap(other)
    edge_grad = call(edge_kernel, shape((rows, width), BF16), dz_one, head, vmem=16)
    other, edge_grad = lax.optimization_barrier((other, edge_grad))
    chip = call(chip_sum_kernel, half, grads, other, vmem=16)
    chip = lax.all_to_all(chip, "dp", 0, 0, axis_index_groups=same_core)
    sums = call(
        owners_sum_kernel,
        shape((peers, 3 * share + SMALL_ROWS, width), BF16),
        chip,
        vmem=16,
    )
    sums = lax.all_to_all(sums, "graph", 0, 0)
    pair, down_grad, basis_grad, up, first, second = call(
        peers_sum_kernel,
        (
            shape((share, width), F32),
            shape((share, trip), F32),
            shape((1, trip), F32),
            shape((up_rows, width), F32),
            shape((share, width), F32),
            shape((share, width), F32),
        ),
        sums,
        vmem=16,
    )
    return edge_grad, pair, down_grad, basis_grad, up, first, second


def solution(mesh):
    split = P(("dp", "graph"), None)
    line = P(("dp", "graph"))
    rows = P("dp", None)
    return jax.shard_map(
        on_device,
        mesh=mesh,
        in_specs=(split, split, P(None, ("dp", "graph")), line, line) + (rows,) * 6,
        out_specs=(split,) + (rows,) * 6,
        check_vma=False,
    )
```

```python
import functools
import math

import jax
import jax.numpy as jnp
from jax import lax
from jax.experimental import pallas as pl
from jax.experimental.pallas import tpu as pltpu
from jax.sharding import PartitionSpec as P

F32 = jnp.float32
BF16 = jnp.bfloat16
SCALE = math.sqrt(0.5)
NT = (((1,), (1,)), ((), ()))
TN = (((0,), (0,)), ((), ()))
LANES = 128
SMALL_ROWS = 16
CHUNK = 256
GROUP = 20
LINES = 16
PIECE = 512
MIB = 1024 * 1024


def dot(a, b, dims=(((1,), (0,)), ((), ()))):
    return lax.dot_general(a, b, dims, preferred_element_type=F32)


def silu_and_slope(value):
    sig = jax.nn.sigmoid(value)
    return value * sig, sig * (1.0 + value * (1.0 - sig))


def iota(shape, dim):
    return lax.broadcasted_iota(jnp.int32, shape, dim)


def one_hot(index_row, rows):
    hit = iota((rows, index_row.shape[1]), 0) == index_row
    return jnp.where(hit, 1.0, 0.0).astype(BF16)


def spread(value, part_row, parts):
    return jnp.concatenate(
        [jnp.where(part_row == part, value, 0.0) for part in range(parts)], axis=0
    ).astype(BF16)


def pick(stack, part_row, parts):
    width = stack.shape[0] // parts
    total = stack[:width]
    for part in range(1, parts):
        total = jnp.where(part_row == part, stack[part * width : (part + 1) * width], total)
    return total


def call(kernel, out_shape, *operands, scratch=(), vmem=32, smem=(), hbm=(), lazy=()):
    fetched = tuple(hbm) + tuple(lazy)

    def body(*refs):
        refs = list(refs)
        sems = refs.pop()
        places = refs[len(refs) - len(fetched) :]
        refs = refs[: len(refs) - len(fetched)]
        copies = []
        for k, (operand, place) in enumerate(zip(fetched, places)):
            copies.append(pltpu.make_async_copy(refs[operand], place, sems.at[k]))
            copies[-1].start()
            refs[operand] = place
        for copy in copies[: len(hbm)]:
            copy.wait()

        def ready():
            for copy in copies[len(hbm) :]:
                copy.wait()

        if lazy:
            kernel(ready, *refs)
        else:
            kernel(*refs)

    def space(k):
        return pltpu.SMEM if k in smem else pltpu.HBM if k in fetched else pltpu.VMEM

    return pl.pallas_call(
        body if fetched else kernel,
        out_shape=out_shape,
        in_specs=[pl.BlockSpec(memory_space=space(k)) for k in range(len(operands))],
        out_specs=jax.tree.map(lambda _: pl.BlockSpec(memory_space=pltpu.VMEM), out_shape),
        scratch_shapes=list(scratch)
        + [pltpu.VMEM(operands[k].shape, operands[k].dtype) for k in fetched]
        + [pltpu.SemaphoreType.DMA((len(fetched),))] * bool(fetched),
        compiler_params=pltpu.CompilerParams(vmem_limit_bytes=vmem * MIB),
    )(*operands)


def order_kernel(peers, e_dev, source_ref, target_ref, basis_ref, rows_ref, sorted_ref, owner_ref, pos, acc):
    lines, lanes = source_ref.shape
    source = source_ref[...]
    peer = source // e_dev
    hits = jnp.concatenate(
        [jnp.where(peer == p, 1.0, 0.0) for p in range(peers)], axis=0
    ).astype(BF16)
    full = peers * lines
    row, col = iota((lanes, lanes), 0), iota((lanes, lanes), 1)
    before = dot(hits, jnp.where(row < col, 1.0, 0.0).astype(BF16))
    count = dot(hits, jnp.ones((lanes, LANES), BF16)).astype(BF16)
    row, col = iota((full, full), 0), iota((full, full), 1)
    same = row // lines == col // lines
    line_start = dot(jnp.where(same & (col < row), 1.0, 0.0).astype(BF16), count)
    in_peer = dot(jnp.where(same, 1.0, 0.0).astype(BF16), count)
    chunks = (in_peer.astype(jnp.int32) + (CHUNK - 1)) // CHUNK
    first_line = (col // lines < row // lines) & (col % lines == 0)
    first_chunk = dot(
        jnp.where(first_line, 1.0, 0.0).astype(BF16), chunks.astype(F32).astype(BF16)
    ).astype(jnp.int32)
    at = iota((1, LANES), 1)
    owner = jnp.zeros((1, LANES), jnp.int32)
    start = (first_chunk * CHUNK).astype(F32) + line_start
    total = jnp.zeros((lines, lanes), F32)
    for p in range(peers):
        block = slice(p * lines, (p + 1) * lines)
        wide = jnp.concatenate([start[block]] * (lanes // LANES), axis=1)
        total = jnp.where(peer == p, wide + before[block], total)
        if p > 0:
            owner += jnp.where(first_chunk[p * lines : p * lines + 1, :] <= at, 1, 0)
    owner_ref[...] = owner
    pos[...] = total.astype(jnp.int32)

    width = LINES * lanes
    pieces = sorted_ref.shape[1] // PIECE
    nb = basis_ref.shape[0]
    extra = 8

    def line(ref, step):
        return jnp.concatenate(
            [ref[pl.ds(step * LINES + k, 1), :] for k in range(LINES)], axis=1
        )

    acc[...] = jnp.zeros_like(acc)

    def place(step, carry):
        here = line(pos, step)
        src = line(source_ref, step) & (e_dev - 1)
        tgt = line(target_ref, step)
        cols = pl.ds(pl.multiple_of(step * width, width), width)
        index = jnp.concatenate(
            [src % CHUNK, src // CHUNK, tgt % CHUNK, tgt // CHUNK]
            + [jnp.zeros((extra - 4, width), jnp.int32)],
            axis=0,
        )
        value = jnp.concatenate([basis_ref[:, cols].astype(F32), index.astype(F32)], axis=0)
        acc[...] += dot(spread(value, here // PIECE, pieces), one_hot(here % PIECE, PIECE), NT)
        return carry

    lax.fori_loop(0, lines // LINES, place, 0)
    for piece in range(pieces):
        cols = slice(piece * PIECE, (piece + 1) * PIECE)
        base = piece * (nb + extra)
        sorted_ref[:, cols] = acc[base : base + nb, :].astype(BF16)
        rows_ref[:, cols] = acc[base + nb : base + nb + extra, :].astype(jnp.int32)


def rows_of(owner, share):
    return pl.ds(pl.multiple_of(owner * share, share), share)


def middle_kernel(
    slot_ref,
    core_ref,
    down_ref,
    rows_ref,
    basis_ref,
    own_ref,
    other_ref,
    cot_ref,
    partial_ref,
    early_ref,
    early_other_ref,
    up_grad_ref,
    basis_grad_ref,
    w_first_s,
    w_second_s,
    up_s,
    basis_s,
    agg_acc,
    agg_s,
    mixed_s,
    inner_s,
    dz_four_s,
    dz_three_s,
    dz_two_s,
    dagg_s,
    down_in_s,
    coeff_s,
    total,
):
    peers, stack_rows, e_hi = down_ref.shape
    slots = rows_ref.shape[1]
    pairs = own_ref.shape[0]
    parts = mixed_s.shape[0] // e_hi
    trip = stack_rows // parts
    width = GROUP * CHUNK
    share = w_first_s.shape[0] // (2 * pairs)
    up_rows = up_s.shape[1]
    core = core_ref[0]

    for pair in range(pairs):
        for ref, side in ((own_ref, core), (other_ref, 1 - core)):
            owner = 2 * pair + side
            w_second_s[rows_of(owner, share), :] = ref[pair, share : 2 * share, :]
            w_first_s[rows_of(owner, share), :] = ref[pair, 2 * share : 3 * share, :]
            small = ref[pair, 3 * share :, :].astype(F32)
            up_s[owner] = small[:up_rows]
            basis_s[owner] = small[up_rows : up_rows + 1, :LANES]
    w_up = jnp.concatenate([up_s[k] for k in range(2 * pairs)], axis=0).astype(BF16)
    w_basis = jnp.concatenate([basis_s[k] for k in range(2 * pairs)], axis=0)
    w_basis = w_basis.T[:trip].astype(BF16)
    agg_acc[...] = jnp.zeros_like(agg_acc)

    def forward(step, carry):
        cols = pl.ds(pl.multiple_of(step * width, width), width)
        found = []
        for k in range(GROUP):
            here = pl.ds(pl.multiple_of(step * width + k * CHUNK, CHUNK), CHUNK)
            slot = slot_ref[0, step * GROUP + k]
            hot = one_hot(rows_ref[0:1, here], e_hi)
            found.append(pick(dot(down_ref[slot], hot), rows_ref[1:2, here], parts))
        down_in = jnp.concatenate(found, axis=1)
        coeff = dot(w_basis, basis_ref[:, cols])
        down_in_s[:, cols] = down_in.astype(BF16)
        coeff_s[:, cols] = coeff
        hot_e = one_hot(rows_ref[2:3, cols], e_hi)
        placed = spread(down_in * coeff, rows_ref[3:4, cols], parts)
        agg_acc[...] += dot(hot_e, placed, NT)
        return carry

    lax.fori_loop(0, slots // width, forward, 0)

    w_first = w_first_s[...]
    w_second = w_second_s[...]
    for q in range(parts):
        rows = slice(q * e_hi, (q + 1) * e_hi)
        agg_s[rows, :] = agg_acc[:, q * trip : (q + 1) * trip].astype(BF16)
    step = 2 * e_hi
    for start in range(0, mixed_s.shape[0], step):
        rows = slice(start, start + step)
        act, slope_two = silu_and_slope(dot(agg_s[rows, :], w_up))
        mixed = act.astype(BF16)
        mixed_s[rows, :] = mixed
        act, slope_three = silu_and_slope(dot(mixed, w_first))
        inner = act.astype(BF16)
        inner_s[rows, :] = inner
        slope_four = silu_and_slope(dot(inner, w_second))[1]
        cot = SCALE * cot_ref[rows, :].astype(F32)
        dz_four = (cot * slope_four).astype(BF16)
        dz_four_s[rows, :] = dz_four
        dz_three = (dot(dz_four, w_second, NT) * slope_three).astype(BF16)
        dz_three_s[rows, :] = dz_three
        dz_two_s[rows, :] = ((cot + dot(dz_three, w_first, NT)) * slope_two).astype(BF16)
    for q in range(parts):
        rows = slice(q * e_hi, (q + 1) * e_hi)
        dagg_s[q * trip : (q + 1) * trip, :] = dot(w_up, dz_two_s[rows, :], NT).astype(BF16)

    w_second_s[...] = dot(inner_s[...], dz_four_s[...], TN).astype(BF16)
    w_first_s[...] = dot(mixed_s[...], dz_three_s[...], TN).astype(BF16)
    up_grad_ref[...] = dot(agg_s[...], dz_two_s[...], TN)
    for pair in range(pairs):
        for ref, side in ((early_ref, core), (early_other_ref, 1 - core)):
            at = rows_of(2 * pair + side, share)
            ref[pair, :share, :] = w_second_s[at, :]
            ref[pair, share:, :] = w_first_s[at, :]

    basis_grad_ref[...] = jnp.zeros_like(basis_grad_ref)
    total[...] = jnp.zeros_like(total)

    def backward(step, carry):
        cols = pl.ds(pl.multiple_of(step * width, width), width)
        hot_e = one_hot(rows_ref[2:3, cols], e_hi)
        dagg_out = pick(dot(dagg_s[...], hot_e), rows_ref[3:4, cols], parts)
        dcoeff = (dagg_out * down_in_s[:, cols].astype(F32)).astype(BF16)
        basis_grad_ref[...] += dot(basis_ref[:, cols], dcoeff, NT)
        placed = spread(dagg_out * coeff_s[:, cols], rows_ref[1:2, cols], parts)
        hot = one_hot(rows_ref[0:1, cols], e_hi)
        terms = []
        for k in range(GROUP):
            here = slice(k * CHUNK, (k + 1) * CHUNK)
            terms.append(dot(placed[:, here], hot[:, here], NT))
        for k in range(GROUP):
            total[slot_ref[0, step * GROUP + k]] += terms[k]
        return carry

    lax.fori_loop(0, slots // width, backward, 0)
    partial_ref[...] = total[...].astype(BF16)


def order(source, target, basis, peers, e_dev):
    shape = jax.ShapeDtypeStruct
    trips = source.shape[0]
    slots = trips + peers * CHUNK
    nb = basis.shape[0]
    lines = trips // LANES
    return call(
        functools.partial(order_kernel, peers, e_dev),
        (shape((8, slots), jnp.int32), shape((nb, slots), BF16), shape((1, LANES), jnp.int32)),
        source.reshape(lines, LANES),
        target.reshape(lines, LANES),
        basis,
        scratch=[
            pltpu.VMEM((lines, LANES), jnp.int32),
            pltpu.VMEM((slots // PIECE * (nb + 8), PIECE), F32),
        ],
        vmem=32,
    )


def middle(slot, core, down, rows, basis, own, other, cot):
    shape = jax.ShapeDtypeStruct
    vmem = pltpu.VMEM
    edges, width = cot.shape
    peers, stack_rows, e_hi = down.shape
    trip = stack_rows * e_hi // edges
    nb = basis.shape[0]
    slots = rows.shape[1]
    half = shape((nb // 2, 2 * width // nb, width), BF16)
    return call(
        middle_kernel,
        (shape(down.shape, BF16), half, half, shape((trip, width), F32), shape((nb, trip), F32)),
        slot,
        core,
        down,
        rows,
        basis,
        own,
        other,
        cot,
        scratch=[
            vmem((width, width), BF16),
            vmem((width, width), BF16),
            vmem((nb, trip // nb, width), F32),
            vmem((nb, 1, LANES), F32),
            vmem((e_hi, stack_rows), F32),
            vmem((edges, trip), BF16),
        ]
        + [vmem((edges, width), BF16)] * 5
        + [
            vmem((stack_rows, e_hi), BF16),
            vmem((trip, slots), BF16),
            vmem((trip, slots), F32),
            vmem(down.shape, F32),
        ],
        smem=(0, 1),
        vmem=44,
    )


def pack_kernel(pair_ref, down_ref, basis_ref, up_ref, first_ref, second_ref, out_ref, small):
    small[...] = jnp.zeros_like(small)
    share = pair_ref.shape[0]
    trip = down_ref.shape[1]
    up_rows = up_ref.shape[0]
    small[:up_rows, :] = up_ref[...].astype(F32)
    small[up_rows : up_rows + 1, :trip] = basis_ref[...].astype(F32)
    place_down(small, down_ref[...].astype(F32))
    rest = small[...].astype(BF16)
    for partner in range(out_ref.shape[0]):
        out_ref[partner, :share, :] = pair_ref[...]
        out_ref[partner, share : 2 * share, :] = second_ref[...]
        out_ref[partner, 2 * share : 3 * share, :] = first_ref[...]
        out_ref[partner, 3 * share :, :] = rest


def place_down(small, down):
    for group in range(down.shape[0] // 8):
        small[8:16, group * LANES : group * LANES + down.shape[1]] = down[
            group * 8 : (group + 1) * 8, :
        ]


def take_down(small, rows, trip):
    return [
        small[8:16, group * LANES : group * LANES + trip] for group in range(rows // 8)
    ]


def down_kernel(core_ref, feats_ref, own_ref, other_ref, down_ref, head_ref):
    rows, width = feats_ref.shape
    peers, stack_rows, block = down_ref.shape
    trip = stack_rows * block // rows
    pairs = own_ref.shape[0]
    share = width // (2 * pairs)
    core = core_ref[0]
    for pair in range(pairs):
        for ref, side in ((own_ref, core), (other_ref, 1 - core)):
            at = pl.ds(pl.multiple_of((2 * pair + side) * share, share), share)
            head_ref[at, :width] = ref[pair, :share, :]
            small = ref[pair, 3 * share :, :].astype(F32)
            down = jnp.concatenate(take_down(small, share, LANES), axis=0)
            head_ref[at, width:] = down.astype(BF16)
    w_pair = head_ref[:, :width]
    w_down = head_ref[:, width : width + trip]
    for part in range(rows // block):
        z_one = dot(feats_ref[part * block : (part + 1) * block, :], w_pair)
        hidden = silu_and_slope(z_one)[0].astype(BF16)
        down_t = dot(hidden, w_down).T.astype(BF16)
        for peer in range(peers):
            down_ref[peer, part * trip : (part + 1) * trip, :] = down_t


def tail_kernel(
    core_ref,
    parts_ref,
    feats_ref,
    weights_ref,
    basis_ref,
    up_ref,
    early_ref,
    early_other_ref,
    dz_ref,
    mine_ref,
    theirs_ref,
    hidden_s,
    ddown_s,
    pair_s,
    small,
):
    peers = parts_ref.shape[0]
    rows, width = feats_ref.shape
    trip = ddown_s.shape[1]
    summed = parts_ref[0].astype(F32)
    for peer in range(1, peers):
        summed += parts_ref[peer].astype(F32)
    span = summed.shape[1]
    for part in range(rows // span):
        ddown_s[part * span : (part + 1) * span, :] = summed[
            part * trip : (part + 1) * trip, :
        ].T.astype(BF16)
    w_down = weights_ref[:, width : width + trip]
    w_pair = weights_ref[:, :width]
    for first in range(0, rows, 512):
        block = slice(first, first + 512)
        act, slope = silu_and_slope(dot(feats_ref[block, :], w_pair))
        hidden_s[block, :] = act.astype(BF16)
        dz_ref[block, :] = (dot(ddown_s[block, :], w_down, NT) * slope).astype(BF16)
    down = dot(hidden_s[...], ddown_s[...], TN)
    pair_s[...] = dot(feats_ref[...], dz_ref[...], TN).astype(BF16)
    owners = basis_ref.shape[0]
    share = width // owners
    up_rows = trip // owners
    small[...] = jnp.zeros_like(small)
    for owner in range(owners):
        small[owner, :up_rows, :] = up_ref[owner * up_rows : (owner + 1) * up_rows, :]
        small[owner, up_rows : up_rows + 1, :trip] = basis_ref[owner : owner + 1, :]
        place_down(small.at[owner], down[owner * share : (owner + 1) * share])
    core = core_ref[0]
    for pair in range(owners // 2):
        for ref, side, half in (
            (mine_ref, core, early_ref),
            (theirs_ref, 1 - core, early_other_ref),
        ):
            owner = 2 * pair + side
            ref[pair, :share, :] = pair_s[rows_of(owner, share), :]
            ref[pair, share : share + SMALL_ROWS, :] = small[owner].astype(BF16)
            ref[pair, share + SMALL_ROWS :, :] = half[pair]


def edge_kernel(dz_ref, weights_ref, out_ref):
    out_ref[...] = dot(dz_ref[...], weights_ref[:, : dz_ref.shape[1]], NT).astype(BF16)


def chip_sum_kernel(own_ref, other_ref, out_ref):
    for pair in range(own_ref.shape[0]):
        total = own_ref[pair].astype(F32) + other_ref[pair].astype(F32)
        out_ref[pair] = total.astype(BF16)


def owners_sum_kernel(parts_ref, out_ref):
    total = parts_ref[0].astype(F32)
    for owner in range(1, parts_ref.shape[0]):
        total += parts_ref[owner].astype(F32)
    total = total.astype(BF16)
    for peer in range(out_ref.shape[0]):
        out_ref[peer] = total


def peers_sum_kernel(parts_ref, pair_ref, down_ref, basis_ref, up_ref, first_ref, second_ref):
    share = pair_ref.shape[0]
    trip = down_ref.shape[1]
    up_rows = up_ref.shape[0]
    total = parts_ref[0].astype(F32)
    for peer in range(1, parts_ref.shape[0]):
        total += parts_ref[peer].astype(F32)
    pair_ref[...] = total[:share]
    small = total[share : share + SMALL_ROWS]
    second_ref[...] = total[share + SMALL_ROWS : 2 * share + SMALL_ROWS]
    first_ref[...] = total[2 * share + SMALL_ROWS :]
    up_ref[...] = small[:up_rows]
    basis_ref[...] = small[up_rows : up_rows + 1, :trip]
    for group, rows in enumerate(take_down(small, share, trip)):
        down_ref[group * 8 : (group + 1) * 8, :] = rows


def on_device(
    edge_feats,
    cotangent,
    angle_basis,
    source_edge,
    target_edge,
    pair_weight,
    down_weight,
    basis_weight,
    up_weight,
    res_first,
    res_second,
):
    shape = jax.ShapeDtypeStruct
    vmem = pltpu.VMEM
    owners = lax.axis_size("dp")
    peers = lax.axis_size("graph")
    pairs = owners // 2
    rows, width = edge_feats.shape
    share = pair_weight.shape[0]
    trip = down_weight.shape[1]
    up_rows = up_weight.shape[0]
    nb = angle_basis.shape[0]
    core = (lax.axis_index("dp") % 2).reshape(1)
    same_core = [[2 * pair + side for pair in range(pairs)] for side in range(2)]

    def swap(value):
        return lax.ppermute(value, "dp", [(owner, owner ^ 1) for owner in range(owners)])

    shards = (pair_weight, down_weight, basis_weight, up_weight, res_first, res_second)
    own = call(
        pack_kernel,
        shape((pairs, 3 * share + SMALL_ROWS, width), BF16),
        pair_weight,
        down_weight,
        basis_weight,
        up_weight,
        res_first,
        res_second,
        scratch=[vmem((SMALL_ROWS, width), F32)],
        hbm=range(6),
        vmem=60,
    )
    own, source_edge = lax.optimization_barrier((own, source_edge))
    own = lax.all_to_all(own, "dp", 0, 0, axis_index_groups=same_core)
    index, basis, slot = order(source_edge, target_edge, angle_basis, peers, rows)
    own, index = lax.optimization_barrier((own, index))
    other = swap(own)
    down, head = call(
        down_kernel,
        (
            shape((peers, rows // CHUNK * trip, CHUNK), BF16),
            shape((width, width + LANES), BF16),
        ),
        core,
        edge_feats,
        own,
        other,
        smem=(0,),
        vmem=16,
    )
    down = lax.all_to_all(down, "graph", 0, 0)
    partial, early, early_other, up_grad, basis_grad = middle(
        slot, core, down, index, basis, own, other, cotangent
    )
    parts = lax.all_to_all(partial, "graph", 0, 0)
    half = shape((pairs, 3 * share + SMALL_ROWS, width), BF16)
    dz_one, grads, other = call(
        tail_kernel,
        (shape((rows, width), BF16), half, half),
        core,
        parts,
        edge_feats,
        head,
        basis_grad,
        up_grad,
        early,
        early_other,
        scratch=[
            vmem((rows, width), BF16),
            vmem((rows, trip), BF16),
            vmem((width, width), BF16),
            vmem((owners, SMALL_ROWS, width), F32),
        ],
        smem=(0,),
        vmem=32,
    )
    other = swap(other)
    edge_grad = call(edge_kernel, shape((rows, width), BF16), dz_one, head, vmem=16)
    other, edge_grad = lax.optimization_barrier((other, edge_grad))
    chip = call(chip_sum_kernel, half, grads, other, vmem=16)
    chip = lax.all_to_all(chip, "dp", 0, 0, axis_index_groups=same_core)
    sums = call(
        owners_sum_kernel,
        shape((peers, 3 * share + SMALL_ROWS, width), BF16),
        chip,
        vmem=16,
    )
    sums = lax.all_to_all(sums, "graph", 0, 0)
    pair, down_grad, basis_grad, up, first, second = call(
        peers_sum_kernel,
        (
            shape((share, width), F32),
            shape((share, trip), F32),
            shape((1, trip), F32),
            shape((up_rows, width), F32),
            shape((share, width), F32),
            shape((share, width), F32),
        ),
        sums,
        vmem=16,
    )
    return edge_grad, pair, down_grad, basis_grad, up, first, second


def solution(mesh):
    split = P(("dp", "graph"), None)
    line = P(("dp", "graph"))
    rows = P("dp", None)
    return jax.shard_map(
        on_device,
        mesh=mesh,
        in_specs=(split, split, P(None, ("dp", "graph")), line, line) + (rows,) * 6,
        out_specs=(split,) + (rows,) * 6,
        check_vma=False,
    )
```

```python
import functools
import math

import jax
import jax.numpy as jnp
from jax import lax
from jax.experimental import pallas as pl
from jax.experimental.pallas import tpu as pltpu
from jax.sharding import PartitionSpec as P

F32 = jnp.float32
BF16 = jnp.bfloat16
SCALE = math.sqrt(0.5)
NT = (((1,), (1,)), ((), ()))
TN = (((0,), (0,)), ((), ()))
LANES = 128
SMALL_ROWS = 16
CHUNK = 256
GROUP = 40
SPAN = 2048
LINES = 16
PIECE = 512
MIB = 1024 * 1024


def dot(a, b, dims=(((1,), (0,)), ((), ()))):
    return lax.dot_general(a, b, dims, preferred_element_type=F32)


def silu_and_slope(value):
    sig = jax.nn.sigmoid(value)
    return value * sig, sig * (1.0 + value * (1.0 - sig))


def iota(shape, dim):
    return lax.broadcasted_iota(jnp.int32, shape, dim)


def one_hot(index_row, rows):
    hit = iota((rows, index_row.shape[1]), 0) == index_row
    return jnp.where(hit, 1.0, 0.0).astype(BF16)


def spread(value, part_row, parts):
    return jnp.concatenate(
        [jnp.where(part_row == part, value, 0.0) for part in range(parts)], axis=0
    ).astype(BF16)


def pick(stack, part_row, parts):
    width = stack.shape[0] // parts
    total = stack[:width]
    for part in range(1, parts):
        total = jnp.where(part_row == part, stack[part * width : (part + 1) * width], total)
    return total


def call(kernel, out_shape, *operands, scratch=(), vmem=32, smem=(), hbm=(), lazy=()):
    fetched = tuple(hbm) + tuple(lazy)

    def body(*refs):
        refs = list(refs)
        sems = refs.pop()
        places = refs[len(refs) - len(fetched) :]
        refs = refs[: len(refs) - len(fetched)]
        copies = []
        for k, (operand, place) in enumerate(zip(fetched, places)):
            copies.append(pltpu.make_async_copy(refs[operand], place, sems.at[k]))
            copies[-1].start()
            refs[operand] = place
        for copy in copies[: len(hbm)]:
            copy.wait()

        def ready():
            for copy in copies[len(hbm) :]:
                copy.wait()

        if lazy:
            kernel(ready, *refs)
        else:
            kernel(*refs)

    def space(k):
        return pltpu.SMEM if k in smem else pltpu.HBM if k in fetched else pltpu.VMEM

    return pl.pallas_call(
        body if fetched else kernel,
        out_shape=out_shape,
        in_specs=[pl.BlockSpec(memory_space=space(k)) for k in range(len(operands))],
        out_specs=jax.tree.map(lambda _: pl.BlockSpec(memory_space=pltpu.VMEM), out_shape),
        scratch_shapes=list(scratch)
        + [pltpu.VMEM(operands[k].shape, operands[k].dtype) for k in fetched]
        + [pltpu.SemaphoreType.DMA((len(fetched),))] * bool(fetched),
        compiler_params=pltpu.CompilerParams(vmem_limit_bytes=vmem * MIB),
    )(*operands)


def order_kernel(peers, e_dev, source_ref, target_ref, basis_ref, rows_ref, sorted_ref, owner_ref, pos, acc):
    lines, lanes = source_ref.shape
    source = source_ref[...]
    peer = source // e_dev
    hits = jnp.concatenate(
        [jnp.where(peer == p, 1.0, 0.0) for p in range(peers)], axis=0
    ).astype(BF16)
    full = peers * lines
    row, col = iota((lanes, lanes), 0), iota((lanes, lanes), 1)
    before = dot(hits, jnp.where(row < col, 1.0, 0.0).astype(BF16))
    count = dot(hits, jnp.ones((lanes, LANES), BF16)).astype(BF16)
    row, col = iota((full, full), 0), iota((full, full), 1)
    same = row // lines == col // lines
    line_start = dot(jnp.where(same & (col < row), 1.0, 0.0).astype(BF16), count)
    in_peer = dot(jnp.where(same, 1.0, 0.0).astype(BF16), count)
    chunks = (in_peer.astype(jnp.int32) + (CHUNK - 1)) // CHUNK
    first_line = (col // lines < row // lines) & (col % lines == 0)
    first_chunk = dot(
        jnp.where(first_line, 1.0, 0.0).astype(BF16), chunks.astype(F32).astype(BF16)
    ).astype(jnp.int32)
    at = iota((1, LANES), 1)
    owner = jnp.zeros((1, LANES), jnp.int32)
    start = (first_chunk * CHUNK).astype(F32) + line_start
    total = jnp.zeros((lines, lanes), F32)
    for p in range(peers):
        block = slice(p * lines, (p + 1) * lines)
        wide = jnp.concatenate([start[block]] * (lanes // LANES), axis=1)
        total = jnp.where(peer == p, wide + before[block], total)
        if p > 0:
            owner += jnp.where(first_chunk[p * lines : p * lines + 1, :] <= at, 1, 0)
    owner_ref[...] = owner
    pos[...] = total.astype(jnp.int32)

    width = LINES * lanes
    pieces = sorted_ref.shape[1] // PIECE
    nb = basis_ref.shape[0]
    extra = 8

    def line(ref, step):
        return jnp.concatenate(
            [ref[pl.ds(step * LINES + k, 1), :] for k in range(LINES)], axis=1
        )

    acc[...] = jnp.zeros_like(acc)

    def place(step, carry):
        here = line(pos, step)
        src = line(source_ref, step) & (e_dev - 1)
        tgt = line(target_ref, step)
        cols = pl.ds(pl.multiple_of(step * width, width), width)
        index = jnp.concatenate(
            [src % CHUNK, src // CHUNK, tgt % CHUNK, tgt // CHUNK]
            + [jnp.zeros((extra - 4, width), jnp.int32)],
            axis=0,
        )
        value = jnp.concatenate([basis_ref[:, cols].astype(F32), index.astype(F32)], axis=0)
        acc[...] += dot(spread(value, here // PIECE, pieces), one_hot(here % PIECE, PIECE), NT)
        return carry

    lax.fori_loop(0, lines // LINES, place, 0)
    for piece in range(pieces):
        cols = slice(piece * PIECE, (piece + 1) * PIECE)
        base = piece * (nb + extra)
        sorted_ref[:, cols] = acc[base : base + nb, :].astype(BF16)
        rows_ref[:, cols] = acc[base + nb : base + nb + extra, :].astype(jnp.int32)


def rows_of(owner, share):
    return pl.ds(pl.multiple_of(owner * share, share), share)


def middle_kernel(
    slot_ref,
    core_ref,
    down_ref,
    rows_ref,
    basis_ref,
    own_ref,
    other_ref,
    cot_ref,
    partial_ref,
    early_ref,
    early_other_ref,
    up_grad_ref,
    basis_grad_ref,
    w_first_s,
    w_second_s,
    up_s,
    basis_s,
    agg_acc,
    agg_s,
    mixed_s,
    inner_s,
    dz_four_s,
    dz_three_s,
    dz_two_s,
    dagg_s,
    down_in_s,
    coeff_s,
    total,
):
    peers, stack_rows, e_hi = down_ref.shape
    slots = rows_ref.shape[1]
    pairs = own_ref.shape[0]
    parts = mixed_s.shape[0] // e_hi
    trip = stack_rows // parts
    width = GROUP * CHUNK
    share = w_first_s.shape[0] // (2 * pairs)
    up_rows = up_s.shape[1]
    core = core_ref[0]

    for pair in range(pairs):
        for ref, side in ((own_ref, core), (other_ref, 1 - core)):
            owner = 2 * pair + side
            w_second_s[rows_of(owner, share), :] = ref[pair, share : 2 * share, :]
            w_first_s[rows_of(owner, share), :] = ref[pair, 2 * share : 3 * share, :]
            small = ref[pair, 3 * share :, :].astype(F32)
            up_s[owner] = small[:up_rows]
            basis_s[owner] = small[up_rows : up_rows + 1, :LANES]
    w_up = jnp.concatenate([up_s[k] for k in range(2 * pairs)], axis=0).astype(BF16)
    w_basis = jnp.concatenate([basis_s[k] for k in range(2 * pairs)], axis=0)
    w_basis = w_basis.T[:trip].astype(BF16)
    agg_acc[...] = jnp.zeros_like(agg_acc)

    def forward(step, carry):
        total_agg = agg_acc[...]
        for first in range(0, width, SPAN):
            cols = pl.ds(pl.multiple_of(step * width + first, SPAN), SPAN)
            found = []
            for k in range(first // CHUNK, (first + SPAN) // CHUNK):
                here = pl.ds(pl.multiple_of(step * width + k * CHUNK, CHUNK), CHUNK)
                slot = slot_ref[0, step * GROUP + k]
                hot = one_hot(rows_ref[0:1, here], e_hi)
                found.append(pick(dot(down_ref[slot], hot), rows_ref[1:2, here], parts))
            down_in = jnp.concatenate(found, axis=1)
            coeff = dot(w_basis, basis_ref[:, cols])
            down_in_s[:, cols] = down_in.astype(BF16)
            coeff_s[:, cols] = coeff
            hot_e = one_hot(rows_ref[2:3, cols], e_hi)
            placed = spread(down_in * coeff, rows_ref[3:4, cols], parts)
            total_agg += dot(hot_e, placed, NT)
        agg_acc[...] = total_agg
        return carry

    lax.fori_loop(0, slots // width, forward, 0)

    w_first = w_first_s[...]
    w_second = w_second_s[...]
    for q in range(parts):
        rows = slice(q * e_hi, (q + 1) * e_hi)
        agg_s[rows, :] = agg_acc[:, q * trip : (q + 1) * trip].astype(BF16)
    step = 2 * e_hi
    for start in range(0, mixed_s.shape[0], step):
        rows = slice(start, start + step)
        act, slope_two = silu_and_slope(dot(agg_s[rows, :], w_up))
        mixed = act.astype(BF16)
        mixed_s[rows, :] = mixed
        act, slope_three = silu_and_slope(dot(mixed, w_first))
        inner = act.astype(BF16)
        inner_s[rows, :] = inner
        slope_four = silu_and_slope(dot(inner, w_second))[1]
        cot = SCALE * cot_ref[rows, :].astype(F32)
        dz_four = (cot * slope_four).astype(BF16)
        dz_four_s[rows, :] = dz_four
        dz_three = (dot(dz_four, w_second, NT) * slope_three).astype(BF16)
        dz_three_s[rows, :] = dz_three
        dz_two_s[rows, :] = ((cot + dot(dz_three, w_first, NT)) * slope_two).astype(BF16)
    for q in range(parts):
        rows = slice(q * e_hi, (q + 1) * e_hi)
        dagg_s[q * trip : (q + 1) * trip, :] = dot(w_up, dz_two_s[rows, :], NT).astype(BF16)

    w_second_s[...] = dot(inner_s[...], dz_four_s[...], TN).astype(BF16)
    w_first_s[...] = dot(mixed_s[...], dz_three_s[...], TN).astype(BF16)
    up_grad_ref[...] = dot(agg_s[...], dz_two_s[...], TN)
    for pair in range(pairs):
        for ref, side in ((early_ref, core), (early_other_ref, 1 - core)):
            at = rows_of(2 * pair + side, share)
            ref[pair, :share, :] = w_second_s[at, :]
            ref[pair, share:, :] = w_first_s[at, :]

    basis_grad_ref[...] = jnp.zeros_like(basis_grad_ref)
    total[...] = jnp.zeros_like(total)

    def backward(step, carry):
        total_basis = basis_grad_ref[...]
        for first in range(0, width, SPAN):
            cols = pl.ds(pl.multiple_of(step * width + first, SPAN), SPAN)
            hot_e = one_hot(rows_ref[2:3, cols], e_hi)
            dagg_out = pick(dot(dagg_s[...], hot_e), rows_ref[3:4, cols], parts)
            dcoeff = (dagg_out * down_in_s[:, cols].astype(F32)).astype(BF16)
            total_basis += dot(basis_ref[:, cols], dcoeff, NT)
            placed = spread(dagg_out * coeff_s[:, cols], rows_ref[1:2, cols], parts)
            hot = one_hot(rows_ref[0:1, cols], e_hi)
            for k in range(SPAN // CHUNK):
                here = slice(k * CHUNK, (k + 1) * CHUNK)
                slot = slot_ref[0, step * GROUP + first // CHUNK + k]
                total[slot] += dot(placed[:, here], hot[:, here], NT)
        basis_grad_ref[...] = total_basis
        return carry

    lax.fori_loop(0, slots // width, backward, 0)
    partial_ref[...] = total[...].astype(BF16)


def order(source, target, basis, peers, e_dev):
    shape = jax.ShapeDtypeStruct
    trips = source.shape[0]
    slots = trips + peers * CHUNK
    nb = basis.shape[0]
    lines = trips // LANES
    return call(
        functools.partial(order_kernel, peers, e_dev),
        (shape((8, slots), jnp.int32), shape((nb, slots), BF16), shape((1, LANES), jnp.int32)),
        source.reshape(lines, LANES),
        target.reshape(lines, LANES),
        basis,
        scratch=[
            pltpu.VMEM((lines, LANES), jnp.int32),
            pltpu.VMEM((slots // PIECE * (nb + 8), PIECE), F32),
        ],
        vmem=32,
    )


def middle(slot, core, down, rows, basis, own, other, cot):
    shape = jax.ShapeDtypeStruct
    vmem = pltpu.VMEM
    edges, width = cot.shape
    peers, stack_rows, e_hi = down.shape
    trip = stack_rows * e_hi // edges
    nb = basis.shape[0]
    slots = rows.shape[1]
    half = shape((nb // 2, 2 * width // nb, width), BF16)
    return call(
        middle_kernel,
        (shape(down.shape, BF16), half, half, shape((trip, width), F32), shape((nb, trip), F32)),
        slot,
        core,
        down,
        rows,
        basis,
        own,
        other,
        cot,
        scratch=[
            vmem((width, width), BF16),
            vmem((width, width), BF16),
            vmem((nb, trip // nb, width), F32),
            vmem((nb, 1, LANES), F32),
            vmem((e_hi, stack_rows), F32),
            vmem((edges, trip), BF16),
        ]
        + [vmem((edges, width), BF16)] * 5
        + [
            vmem((stack_rows, e_hi), BF16),
            vmem((trip, slots), BF16),
            vmem((trip, slots), F32),
            vmem(down.shape, F32),
        ],
        smem=(0, 1),
        vmem=44,
    )


def pack_kernel(pair_ref, down_ref, basis_ref, up_ref, first_ref, second_ref, out_ref, small):
    small[...] = jnp.zeros_like(small)
    share = pair_ref.shape[0]
    trip = down_ref.shape[1]
    up_rows = up_ref.shape[0]
    small[:up_rows, :] = up_ref[...].astype(F32)
    small[up_rows : up_rows + 1, :trip] = basis_ref[...].astype(F32)
    place_down(small, down_ref[...].astype(F32))
    rest = small[...].astype(BF16)
    for partner in range(out_ref.shape[0]):
        out_ref[partner, :share, :] = pair_ref[...]
        out_ref[partner, share : 2 * share, :] = second_ref[...]
        out_ref[partner, 2 * share : 3 * share, :] = first_ref[...]
        out_ref[partner, 3 * share :, :] = rest


def place_down(small, down):
    for group in range(down.shape[0] // 8):
        small[8:16, group * LANES : group * LANES + down.shape[1]] = down[
            group * 8 : (group + 1) * 8, :
        ]


def take_down(small, rows, trip):
    return [
        small[8:16, group * LANES : group * LANES + trip] for group in range(rows // 8)
    ]


def down_kernel(core_ref, feats_ref, own_ref, other_ref, down_ref, head_ref):
    rows, width = feats_ref.shape
    peers, stack_rows, block = down_ref.shape
    trip = stack_rows * block // rows
    pairs = own_ref.shape[0]
    share = width // (2 * pairs)
    core = core_ref[0]
    for pair in range(pairs):
        for ref, side in ((own_ref, core), (other_ref, 1 - core)):
            at = pl.ds(pl.multiple_of((2 * pair + side) * share, share), share)
            head_ref[at, :width] = ref[pair, :share, :]
            small = ref[pair, 3 * share :, :].astype(F32)
            down = jnp.concatenate(take_down(small, share, LANES), axis=0)
            head_ref[at, width:] = down.astype(BF16)
    w_pair = head_ref[:, :width]
    w_down = head_ref[:, width : width + trip]
    for part in range(rows // block):
        z_one = dot(feats_ref[part * block : (part + 1) * block, :], w_pair)
        hidden = silu_and_slope(z_one)[0].astype(BF16)
        down_t = dot(hidden, w_down).T.astype(BF16)
        for peer in range(peers):
            down_ref[peer, part * trip : (part + 1) * trip, :] = down_t


def tail_kernel(
    core_ref,
    parts_ref,
    feats_ref,
    weights_ref,
    basis_ref,
    up_ref,
    early_ref,
    early_other_ref,
    dz_ref,
    mine_ref,
    theirs_ref,
    hidden_s,
    ddown_s,
    pair_s,
    small,
):
    peers = parts_ref.shape[0]
    rows, width = feats_ref.shape
    trip = ddown_s.shape[1]
    summed = parts_ref[0].astype(F32)
    for peer in range(1, peers):
        summed += parts_ref[peer].astype(F32)
    span = summed.shape[1]
    for part in range(rows // span):
        ddown_s[part * span : (part + 1) * span, :] = summed[
            part * trip : (part + 1) * trip, :
        ].T.astype(BF16)
    w_down = weights_ref[:, width : width + trip]
    w_pair = weights_ref[:, :width]
    for first in range(0, rows, 512):
        block = slice(first, first + 512)
        act, slope = silu_and_slope(dot(feats_ref[block, :], w_pair))
        hidden_s[block, :] = act.astype(BF16)
        dz_ref[block, :] = (dot(ddown_s[block, :], w_down, NT) * slope).astype(BF16)
    down = dot(hidden_s[...], ddown_s[...], TN)
    pair_s[...] = dot(feats_ref[...], dz_ref[...], TN).astype(BF16)
    owners = basis_ref.shape[0]
    share = width // owners
    up_rows = trip // owners
    small[...] = jnp.zeros_like(small)
    for owner in range(owners):
        small[owner, :up_rows, :] = up_ref[owner * up_rows : (owner + 1) * up_rows, :]
        small[owner, up_rows : up_rows + 1, :trip] = basis_ref[owner : owner + 1, :]
        place_down(small.at[owner], down[owner * share : (owner + 1) * share])
    core = core_ref[0]
    for pair in range(owners // 2):
        for ref, side, half in (
            (mine_ref, core, early_ref),
            (theirs_ref, 1 - core, early_other_ref),
        ):
            owner = 2 * pair + side
            ref[pair, :share, :] = pair_s[rows_of(owner, share), :]
            ref[pair, share : share + SMALL_ROWS, :] = small[owner].astype(BF16)
            ref[pair, share + SMALL_ROWS :, :] = half[pair]


def edge_kernel(dz_ref, weights_ref, out_ref):
    out_ref[...] = dot(dz_ref[...], weights_ref[:, : dz_ref.shape[1]], NT).astype(BF16)


def chip_sum_kernel(own_ref, other_ref, out_ref):
    for pair in range(own_ref.shape[0]):
        total = own_ref[pair].astype(F32) + other_ref[pair].astype(F32)
        out_ref[pair] = total.astype(BF16)


def owners_sum_kernel(parts_ref, out_ref):
    total = parts_ref[0].astype(F32)
    for owner in range(1, parts_ref.shape[0]):
        total += parts_ref[owner].astype(F32)
    total = total.astype(BF16)
    for peer in range(out_ref.shape[0]):
        out_ref[peer] = total


def peers_sum_kernel(parts_ref, pair_ref, down_ref, basis_ref, up_ref, first_ref, second_ref):
    share = pair_ref.shape[0]
    trip = down_ref.shape[1]
    up_rows = up_ref.shape[0]
    total = parts_ref[0].astype(F32)
    for peer in range(1, parts_ref.shape[0]):
        total += parts_ref[peer].astype(F32)
    pair_ref[...] = total[:share]
    small = total[share : share + SMALL_ROWS]
    second_ref[...] = total[share + SMALL_ROWS : 2 * share + SMALL_ROWS]
    first_ref[...] = total[2 * share + SMALL_ROWS :]
    up_ref[...] = small[:up_rows]
    basis_ref[...] = small[up_rows : up_rows + 1, :trip]
    for group, rows in enumerate(take_down(small, share, trip)):
        down_ref[group * 8 : (group + 1) * 8, :] = rows


def on_device(
    edge_feats,
    cotangent,
    angle_basis,
    source_edge,
    target_edge,
    pair_weight,
    down_weight,
    basis_weight,
    up_weight,
    res_first,
    res_second,
):
    shape = jax.ShapeDtypeStruct
    vmem = pltpu.VMEM
    owners = lax.axis_size("dp")
    peers = lax.axis_size("graph")
    pairs = owners // 2
    rows, width = edge_feats.shape
    share = pair_weight.shape[0]
    trip = down_weight.shape[1]
    up_rows = up_weight.shape[0]
    nb = angle_basis.shape[0]
    core = (lax.axis_index("dp") % 2).reshape(1)
    same_core = [[2 * pair + side for pair in range(pairs)] for side in range(2)]

    def swap(value):
        return lax.ppermute(value, "dp", [(owner, owner ^ 1) for owner in range(owners)])

    shards = (pair_weight, down_weight, basis_weight, up_weight, res_first, res_second)
    own = call(
        pack_kernel,
        shape((pairs, 3 * share + SMALL_ROWS, width), BF16),
        pair_weight,
        down_weight,
        basis_weight,
        up_weight,
        res_first,
        res_second,
        scratch=[vmem((SMALL_ROWS, width), F32)],
        hbm=range(6),
        vmem=60,
    )
    own, source_edge = lax.optimization_barrier((own, source_edge))
    own = lax.all_to_all(own, "dp", 0, 0, axis_index_groups=same_core)
    index, basis, slot = order(source_edge, target_edge, angle_basis, peers, rows)
    own, index = lax.optimization_barrier((own, index))
    other = swap(own)
    down, head = call(
        down_kernel,
        (
            shape((peers, rows // CHUNK * trip, CHUNK), BF16),
            shape((width, width + LANES), BF16),
        ),
        core,
        edge_feats,
        own,
        other,
        smem=(0,),
        vmem=16,
    )
    down = lax.all_to_all(down, "graph", 0, 0)
    partial, early, early_other, up_grad, basis_grad = middle(
        slot, core, down, index, basis, own, other, cotangent
    )
    parts = lax.all_to_all(partial, "graph", 0, 0)
    half = shape((pairs, 3 * share + SMALL_ROWS, width), BF16)
    dz_one, grads, other = call(
        tail_kernel,
        (shape((rows, width), BF16), half, half),
        core,
        parts,
        edge_feats,
        head,
        basis_grad,
        up_grad,
        early,
        early_other,
        scratch=[
            vmem((rows, width), BF16),
            vmem((rows, trip), BF16),
            vmem((width, width), BF16),
            vmem((owners, SMALL_ROWS, width), F32),
        ],
        smem=(0,),
        vmem=32,
    )
    other = swap(other)
    edge_grad = call(edge_kernel, shape((rows, width), BF16), dz_one, head, vmem=16)
    other, edge_grad = lax.optimization_barrier((other, edge_grad))
    chip = call(chip_sum_kernel, half, grads, other, vmem=16)
    chip = lax.all_to_all(chip, "dp", 0, 0, axis_index_groups=same_core)
    sums = call(
        owners_sum_kernel,
        shape((peers, 3 * share + SMALL_ROWS, width), BF16),
        chip,
        vmem=16,
    )
    sums = lax.all_to_all(sums, "graph", 0, 0)
    pair, down_grad, basis_grad, up, first, second = call(
        peers_sum_kernel,
        (
            shape((share, width), F32),
            shape((share, trip), F32),
            shape((1, trip), F32),
            shape((up_rows, width), F32),
            shape((share, width), F32),
            shape((share, width), F32),
        ),
        sums,
        vmem=16,
    )
    return edge_grad, pair, down_grad, basis_grad, up, first, second


def solution(mesh):
    split = P(("dp", "graph"), None)
    line = P(("dp", "graph"))
    rows = P("dp", None)
    return jax.shard_map(
        on_device,
        mesh=mesh,
        in_specs=(split, split, P(None, ("dp", "graph")), line, line) + (rows,) * 6,
        out_specs=(split,) + (rows,) * 6,
        check_vma=False,
    )
```

```python
import functools
import math

import jax
import jax.numpy as jnp
from jax import lax
from jax.experimental import pallas as pl
from jax.experimental.pallas import tpu as pltpu
from jax.sharding import PartitionSpec as P

F32 = jnp.float32
BF16 = jnp.bfloat16
SCALE = math.sqrt(0.5)
NT = (((1,), (1,)), ((), ()))
TN = (((0,), (0,)), ((), ()))
LANES = 128
SMALL_ROWS = 16
CHUNK = 256
GROUP = 40
SPAN = 2048
LINES = 16
PIECE = 512
MIB = 1024 * 1024


def dot(a, b, dims=(((1,), (0,)), ((), ()))):
    return lax.dot_general(a, b, dims, preferred_element_type=F32)


def silu_and_slope(value):
    sig = jax.nn.sigmoid(value)
    return value * sig, sig * (1.0 + value * (1.0 - sig))


def iota(shape, dim):
    return lax.broadcasted_iota(jnp.int32, shape, dim)


def one_hot(index_row, rows):
    hit = iota((rows, index_row.shape[1]), 0) == index_row
    return jnp.where(hit, 1.0, 0.0).astype(BF16)


def spread(value, part_row, parts):
    return jnp.concatenate(
        [jnp.where(part_row == part, value, 0.0) for part in range(parts)], axis=0
    ).astype(BF16)


def pick(stack, part_row, parts):
    width = stack.shape[0] // parts
    total = stack[:width]
    for part in range(1, parts):
        total = jnp.where(part_row == part, stack[part * width : (part + 1) * width], total)
    return total


def call(kernel, out_shape, *operands, scratch=(), vmem=32, smem=(), hbm=(), lazy=()):
    fetched = tuple(hbm) + tuple(lazy)

    def body(*refs):
        refs = list(refs)
        sems = refs.pop()
        places = refs[len(refs) - len(fetched) :]
        refs = refs[: len(refs) - len(fetched)]
        copies = []
        for k, (operand, place) in enumerate(zip(fetched, places)):
            copies.append(pltpu.make_async_copy(refs[operand], place, sems.at[k]))
            copies[-1].start()
            refs[operand] = place
        for copy in copies[: len(hbm)]:
            copy.wait()

        def ready():
            for copy in copies[len(hbm) :]:
                copy.wait()

        if lazy:
            kernel(ready, *refs)
        else:
            kernel(*refs)

    def space(k):
        return pltpu.SMEM if k in smem else pltpu.HBM if k in fetched else pltpu.VMEM

    return pl.pallas_call(
        body if fetched else kernel,
        out_shape=out_shape,
        in_specs=[pl.BlockSpec(memory_space=space(k)) for k in range(len(operands))],
        out_specs=jax.tree.map(lambda _: pl.BlockSpec(memory_space=pltpu.VMEM), out_shape),
        scratch_shapes=list(scratch)
        + [pltpu.VMEM(operands[k].shape, operands[k].dtype) for k in fetched]
        + [pltpu.SemaphoreType.DMA((len(fetched),))] * bool(fetched),
        compiler_params=pltpu.CompilerParams(vmem_limit_bytes=vmem * MIB),
    )(*operands)


def order_kernel(peers, e_dev, source_ref, target_ref, basis_ref, rows_ref, sorted_ref, owner_ref, pos, acc):
    lines, lanes = source_ref.shape
    source = source_ref[...]
    peer = source // e_dev
    hits = jnp.concatenate(
        [jnp.where(peer == p, 1.0, 0.0) for p in range(peers)], axis=0
    ).astype(BF16)
    full = peers * lines
    row, col = iota((lanes, lanes), 0), iota((lanes, lanes), 1)
    before = dot(hits, jnp.where(row < col, 1.0, 0.0).astype(BF16))
    count = dot(hits, jnp.ones((lanes, LANES), BF16)).astype(BF16)
    row, col = iota((full, full), 0), iota((full, full), 1)
    same = row // lines == col // lines
    line_start = dot(jnp.where(same & (col < row), 1.0, 0.0).astype(BF16), count)
    in_peer = dot(jnp.where(same, 1.0, 0.0).astype(BF16), count)
    chunks = (in_peer.astype(jnp.int32) + (CHUNK - 1)) // CHUNK
    first_line = (col // lines < row // lines) & (col % lines == 0)
    first_chunk = dot(
        jnp.where(first_line, 1.0, 0.0).astype(BF16), chunks.astype(F32).astype(BF16)
    ).astype(jnp.int32)
    at = iota((1, LANES), 1)
    owner = jnp.zeros((1, LANES), jnp.int32)
    start = (first_chunk * CHUNK).astype(F32) + line_start
    total = jnp.zeros((lines, lanes), F32)
    for p in range(peers):
        block = slice(p * lines, (p + 1) * lines)
        wide = jnp.concatenate([start[block]] * (lanes // LANES), axis=1)
        total = jnp.where(peer == p, wide + before[block], total)
        if p > 0:
            owner += jnp.where(first_chunk[p * lines : p * lines + 1, :] <= at, 1, 0)
    owner_ref[...] = owner
    pos[...] = total.astype(jnp.int32)

    width = LINES * lanes
    pieces = sorted_ref.shape[1] // PIECE
    nb = basis_ref.shape[0]
    extra = 8

    def line(ref, step):
        return jnp.concatenate(
            [ref[pl.ds(step * LINES + k, 1), :] for k in range(LINES)], axis=1
        )

    acc[...] = jnp.zeros_like(acc)

    def place(step, carry):
        here = line(pos, step)
        src = line(source_ref, step) & (e_dev - 1)
        tgt = line(target_ref, step)
        cols = pl.ds(pl.multiple_of(step * width, width), width)
        index = jnp.concatenate(
            [src % CHUNK, src // CHUNK, tgt % CHUNK, tgt // CHUNK]
            + [jnp.zeros((extra - 4, width), jnp.int32)],
            axis=0,
        )
        value = jnp.concatenate([basis_ref[:, cols].astype(F32), index.astype(F32)], axis=0)
        acc[...] += dot(spread(value, here // PIECE, pieces), one_hot(here % PIECE, PIECE), NT)
        return carry

    lax.fori_loop(0, lines // LINES, place, 0)
    for piece in range(pieces):
        cols = slice(piece * PIECE, (piece + 1) * PIECE)
        base = piece * (nb + extra)
        sorted_ref[:, cols] = acc[base : base + nb, :].astype(BF16)
        rows_ref[:, cols] = acc[base + nb : base + nb + extra, :].astype(jnp.int32)


def rows_of(owner, share):
    return pl.ds(pl.multiple_of(owner * share, share), share)


def middle_kernel(
    slot_ref,
    core_ref,
    down_ref,
    rows_ref,
    basis_ref,
    own_ref,
    other_ref,
    cot_ref,
    partial_ref,
    early_ref,
    early_other_ref,
    up_grad_ref,
    basis_grad_ref,
    w_first_s,
    w_second_s,
    up_s,
    basis_s,
    agg_acc,
    agg_s,
    mixed_s,
    inner_s,
    dz_four_s,
    dz_three_s,
    dz_two_s,
    dagg_s,
    down_in_s,
    coeff_s,
    total,
):
    peers, stack_rows, e_hi = down_ref.shape
    slots = rows_ref.shape[1]
    pairs = own_ref.shape[0]
    parts = mixed_s.shape[0] // e_hi
    trip = stack_rows // parts
    width = GROUP * CHUNK
    share = w_first_s.shape[0] // (2 * pairs)
    up_rows = up_s.shape[1]
    core = core_ref[0]

    for pair in range(pairs):
        for ref, side in ((own_ref, core), (other_ref, 1 - core)):
            owner = 2 * pair + side
            w_second_s[rows_of(owner, share), :] = ref[pair, share : 2 * share, :]
            w_first_s[rows_of(owner, share), :] = ref[pair, 2 * share : 3 * share, :]
            small = ref[pair, 3 * share :, :].astype(F32)
            up_s[owner] = small[:up_rows]
            basis_s[owner] = small[up_rows : up_rows + 1, :LANES]
    w_up = jnp.concatenate([up_s[k] for k in range(2 * pairs)], axis=0).astype(BF16)
    w_basis = jnp.concatenate([basis_s[k] for k in range(2 * pairs)], axis=0)
    w_basis = w_basis.T[:trip].astype(BF16)
    agg_acc[...] = jnp.zeros_like(agg_acc)

    def forward(step, carry):
        total_agg = agg_acc[...]
        for first in range(0, width, SPAN):
            cols = pl.ds(pl.multiple_of(step * width + first, SPAN), SPAN)
            found = []
            for k in range(first // CHUNK, (first + SPAN) // CHUNK):
                here = pl.ds(pl.multiple_of(step * width + k * CHUNK, CHUNK), CHUNK)
                slot = slot_ref[0, step * GROUP + k]
                hot = one_hot(rows_ref[0:1, here], e_hi)
                found.append(pick(dot(down_ref[slot], hot), rows_ref[1:2, here], parts))
            down_in = jnp.concatenate(found, axis=1)
            coeff = dot(w_basis, basis_ref[:, cols])
            down_in_s[:, cols] = down_in.astype(BF16)
            coeff_s[:, cols] = coeff
            hot_e = one_hot(rows_ref[2:3, cols], e_hi)
            placed = spread(down_in * coeff, rows_ref[3:4, cols], parts)
            total_agg += dot(hot_e, placed, NT)
        agg_acc[...] = total_agg
        return carry

    lax.fori_loop(0, slots // width, forward, 0)

    w_first = w_first_s[...]
    w_second = w_second_s[...]
    for q in range(parts):
        rows = slice(q * e_hi, (q + 1) * e_hi)
        agg_s[rows, :] = agg_acc[:, q * trip : (q + 1) * trip].astype(BF16)
    step = 2 * e_hi
    for start in range(0, mixed_s.shape[0], step):
        rows = slice(start, start + step)
        act, slope_two = silu_and_slope(dot(agg_s[rows, :], w_up))
        mixed = act.astype(BF16)
        mixed_s[rows, :] = mixed
        act, slope_three = silu_and_slope(dot(mixed, w_first))
        inner = act.astype(BF16)
        inner_s[rows, :] = inner
        slope_four = silu_and_slope(dot(inner, w_second))[1]
        cot = SCALE * cot_ref[rows, :].astype(F32)
        dz_four = (cot * slope_four).astype(BF16)
        dz_four_s[rows, :] = dz_four
        dz_three = (dot(dz_four, w_second, NT) * slope_three).astype(BF16)
        dz_three_s[rows, :] = dz_three
        dz_two_s[rows, :] = ((cot + dot(dz_three, w_first, NT)) * slope_two).astype(BF16)
    for q in range(parts):
        rows = slice(q * e_hi, (q + 1) * e_hi)
        dagg_s[q * trip : (q + 1) * trip, :] = dot(w_up, dz_two_s[rows, :], NT).astype(BF16)

    w_second_s[...] = dot(inner_s[...], dz_four_s[...], TN).astype(BF16)
    w_first_s[...] = dot(mixed_s[...], dz_three_s[...], TN).astype(BF16)
    up_grad_ref[...] = dot(agg_s[...], dz_two_s[...], TN)
    for pair in range(pairs):
        for ref, side in ((early_ref, core), (early_other_ref, 1 - core)):
            at = rows_of(2 * pair + side, share)
            ref[pair, :share, :] = w_second_s[at, :]
            ref[pair, share:, :] = w_first_s[at, :]

    basis_grad_ref[...] = jnp.zeros_like(basis_grad_ref)
    total[...] = jnp.zeros_like(total)

    def backward(step, carry):
        total_basis = basis_grad_ref[...]
        for first in range(0, width, SPAN):
            cols = pl.ds(pl.multiple_of(step * width + first, SPAN), SPAN)
            hot_e = one_hot(rows_ref[2:3, cols], e_hi)
            dagg_out = pick(dot(dagg_s[...], hot_e), rows_ref[3:4, cols], parts)
            dcoeff = (dagg_out * down_in_s[:, cols].astype(F32)).astype(BF16)
            total_basis += dot(basis_ref[:, cols], dcoeff, NT)
            placed = spread(dagg_out * coeff_s[:, cols], rows_ref[1:2, cols], parts)
            hot = one_hot(rows_ref[0:1, cols], e_hi)
            for k in range(SPAN // CHUNK):
                here = slice(k * CHUNK, (k + 1) * CHUNK)
                slot = slot_ref[0, step * GROUP + first // CHUNK + k]
                total[slot] += dot(placed[:, here], hot[:, here], NT)
        basis_grad_ref[...] = total_basis
        return carry

    lax.fori_loop(0, slots // width, backward, 0)
    partial_ref[...] = total[...].astype(BF16)


def order(source, target, basis, peers, e_dev):
    shape = jax.ShapeDtypeStruct
    trips = source.shape[0]
    slots = trips + peers * CHUNK
    nb = basis.shape[0]
    lines = trips // LANES
    return call(
        functools.partial(order_kernel, peers, e_dev),
        (shape((8, slots), jnp.int32), shape((nb, slots), BF16), shape((1, LANES), jnp.int32)),
        source.reshape(lines, LANES),
        target.reshape(lines, LANES),
        basis,
        scratch=[
            pltpu.VMEM((lines, LANES), jnp.int32),
            pltpu.VMEM((slots // PIECE * (nb + 8), PIECE), F32),
        ],
        vmem=32,
    )


def middle(slot, core, down, rows, basis, own, other, cot):
    shape = jax.ShapeDtypeStruct
    vmem = pltpu.VMEM
    edges, width = cot.shape
    peers, stack_rows, e_hi = down.shape
    trip = stack_rows * e_hi // edges
    nb = basis.shape[0]
    slots = rows.shape[1]
    half = shape((nb // 2, 2 * width // nb, width), BF16)
    return call(
        middle_kernel,
        (shape(down.shape, BF16), half, half, shape((trip, width), F32), shape((nb, trip), F32)),
        slot,
        core,
        down,
        rows,
        basis,
        own,
        other,
        cot,
        scratch=[
            vmem((width, width), BF16),
            vmem((width, width), BF16),
            vmem((nb, trip // nb, width), F32),
            vmem((nb, 1, LANES), F32),
            vmem((e_hi, stack_rows), F32),
            vmem((edges, trip), BF16),
        ]
        + [vmem((edges, width), BF16)] * 5
        + [
            vmem((stack_rows, e_hi), BF16),
            vmem((trip, slots), BF16),
            vmem((trip, slots), F32),
            vmem(down.shape, F32),
        ],
        smem=(0, 1),
        vmem=44,
    )


def pack_kernel(pair_ref, down_ref, basis_ref, up_ref, first_ref, second_ref, out_ref, small):
    small[...] = jnp.zeros_like(small)
    share = pair_ref.shape[0]
    trip = down_ref.shape[1]
    up_rows = up_ref.shape[0]
    small[:up_rows, :] = up_ref[...].astype(F32)
    small[up_rows : up_rows + 1, :trip] = basis_ref[...].astype(F32)
    place_down(small, down_ref[...].astype(F32))
    rest = small[...].astype(BF16)
    for partner in range(out_ref.shape[0]):
        out_ref[partner, :share, :] = pair_ref[...]
        out_ref[partner, share : 2 * share, :] = second_ref[...]
        out_ref[partner, 2 * share : 3 * share, :] = first_ref[...]
        out_ref[partner, 3 * share :, :] = rest


def place_down(small, down):
    for group in range(down.shape[0] // 8):
        small[8:16, group * LANES : group * LANES + down.shape[1]] = down[
            group * 8 : (group + 1) * 8, :
        ]


def take_down(small, rows, trip):
    return [
        small[8:16, group * LANES : group * LANES + trip] for group in range(rows // 8)
    ]


def down_kernel(core_ref, feats_ref, own_ref, other_ref, down_ref, head_ref):
    rows, width = feats_ref.shape
    peers, stack_rows, block = down_ref.shape
    trip = stack_rows * block // rows
    pairs = own_ref.shape[0]
    share = width // (2 * pairs)
    core = core_ref[0]
    for pair in range(pairs):
        for ref, side in ((own_ref, core), (other_ref, 1 - core)):
            at = pl.ds(pl.multiple_of((2 * pair + side) * share, share), share)
            head_ref[at, :width] = ref[pair, :share, :]
            small = ref[pair, 3 * share :, :].astype(F32)
            down = jnp.concatenate(take_down(small, share, LANES), axis=0)
            head_ref[at, width:] = down.astype(BF16)
    w_pair = head_ref[:, :width]
    w_down = head_ref[:, width : width + trip]
    for part in range(rows // block):
        z_one = dot(feats_ref[part * block : (part + 1) * block, :], w_pair)
        hidden = silu_and_slope(z_one)[0].astype(BF16)
        down_t = dot(hidden, w_down).T.astype(BF16)
        for peer in range(peers):
            down_ref[peer, part * trip : (part + 1) * trip, :] = down_t


def tail_kernel(
    core_ref,
    parts_ref,
    feats_ref,
    weights_ref,
    basis_ref,
    up_ref,
    early_ref,
    early_other_ref,
    dz_ref,
    mine_ref,
    theirs_ref,
    hidden_s,
    ddown_s,
    pair_s,
    small,
):
    peers = parts_ref.shape[0]
    rows, width = feats_ref.shape
    trip = ddown_s.shape[1]
    summed = parts_ref[0].astype(F32)
    for peer in range(1, peers):
        summed += parts_ref[peer].astype(F32)
    span = summed.shape[1]
    for part in range(rows // span):
        ddown_s[part * span : (part + 1) * span, :] = summed[
            part * trip : (part + 1) * trip, :
        ].T.astype(BF16)
    w_down = weights_ref[:, width : width + trip]
    w_pair = weights_ref[:, :width]
    for first in range(0, rows, 512):
        block = slice(first, first + 512)
        act, slope = silu_and_slope(dot(feats_ref[block, :], w_pair))
        hidden_s[block, :] = act.astype(BF16)
        dz_ref[block, :] = (dot(ddown_s[block, :], w_down, NT) * slope).astype(BF16)
    down = dot(hidden_s[...], ddown_s[...], TN)
    pair_s[...] = dot(feats_ref[...], dz_ref[...], TN).astype(BF16)
    owners = basis_ref.shape[0]
    share = width // owners
    up_rows = trip // owners
    small[...] = jnp.zeros_like(small)
    for owner in range(owners):
        small[owner, :up_rows, :] = up_ref[owner * up_rows : (owner + 1) * up_rows, :]
        small[owner, up_rows : up_rows + 1, :trip] = basis_ref[owner : owner + 1, :]
        place_down(small.at[owner], down[owner * share : (owner + 1) * share])
    core = core_ref[0]
    for pair in range(owners // 2):
        for ref, side, half in (
            (mine_ref, core, early_ref),
            (theirs_ref, 1 - core, early_other_ref),
        ):
            owner = 2 * pair + side
            ref[pair, :share, :] = pair_s[rows_of(owner, share), :]
            ref[pair, share : share + SMALL_ROWS, :] = small[owner].astype(BF16)
            ref[pair, share + SMALL_ROWS :, :] = half[pair]


def edge_kernel(dz_ref, weights_ref, out_ref):
    out_ref[...] = dot(dz_ref[...], weights_ref[:, : dz_ref.shape[1]], NT).astype(BF16)


def chip_sum_kernel(own_ref, other_ref, out_ref):
    for pair in range(own_ref.shape[0]):
        total = own_ref[pair].astype(F32) + other_ref[pair].astype(F32)
        out_ref[pair] = total.astype(BF16)


def owners_sum_kernel(parts_ref, out_ref):
    total = parts_ref[0].astype(F32)
    for owner in range(1, parts_ref.shape[0]):
        total += parts_ref[owner].astype(F32)
    total = total.astype(BF16)
    out_ref[...] = total


def pair_sum_kernel(own_ref, other_ref, out_ref):
    total = (own_ref[...].astype(F32) + other_ref[...].astype(F32)).astype(BF16)
    for peer in range(out_ref.shape[0]):
        out_ref[peer] = total


def peers_sum_kernel(parts_ref, pair_ref, down_ref, basis_ref, up_ref, first_ref, second_ref):
    share = pair_ref.shape[0]
    trip = down_ref.shape[1]
    up_rows = up_ref.shape[0]
    total = parts_ref[0].astype(F32)
    for peer in range(1, parts_ref.shape[0]):
        total += parts_ref[peer].astype(F32)
    pair_ref[...] = total[:share]
    small = total[share : share + SMALL_ROWS]
    second_ref[...] = total[share + SMALL_ROWS : 2 * share + SMALL_ROWS]
    first_ref[...] = total[2 * share + SMALL_ROWS :]
    up_ref[...] = small[:up_rows]
    basis_ref[...] = small[up_rows : up_rows + 1, :trip]
    for group, rows in enumerate(take_down(small, share, trip)):
        down_ref[group * 8 : (group + 1) * 8, :] = rows


def on_device(
    edge_feats,
    cotangent,
    angle_basis,
    source_edge,
    target_edge,
    pair_weight,
    down_weight,
    basis_weight,
    up_weight,
    res_first,
    res_second,
):
    shape = jax.ShapeDtypeStruct
    vmem = pltpu.VMEM
    owners = lax.axis_size("dp")
    peers = lax.axis_size("graph")
    pairs = owners // 2
    rows, width = edge_feats.shape
    share = pair_weight.shape[0]
    trip = down_weight.shape[1]
    up_rows = up_weight.shape[0]
    nb = angle_basis.shape[0]
    core = (lax.axis_index("dp") % 2).reshape(1)
    same_core = [[2 * pair + side for pair in range(pairs)] for side in range(2)]

    def swap(value):
        return lax.ppermute(value, "dp", [(owner, owner ^ 1) for owner in range(owners)])

    shards = (pair_weight, down_weight, basis_weight, up_weight, res_first, res_second)
    own = call(
        pack_kernel,
        shape((pairs, 3 * share + SMALL_ROWS, width), BF16),
        pair_weight,
        down_weight,
        basis_weight,
        up_weight,
        res_first,
        res_second,
        scratch=[vmem((SMALL_ROWS, width), F32)],
        hbm=range(6),
        vmem=60,
    )
    own, source_edge = lax.optimization_barrier((own, source_edge))
    own = lax.all_to_all(own, "dp", 0, 0, axis_index_groups=same_core)
    index, basis, slot = order(source_edge, target_edge, angle_basis, peers, rows)
    own, index = lax.optimization_barrier((own, index))
    other = swap(own)
    down, head = call(
        down_kernel,
        (
            shape((peers, rows // CHUNK * trip, CHUNK), BF16),
            shape((width, width + LANES), BF16),
        ),
        core,
        edge_feats,
        own,
        other,
        smem=(0,),
        vmem=16,
    )
    down = lax.all_to_all(down, "graph", 0, 0)
    partial, early, early_other, up_grad, basis_grad = middle(
        slot, core, down, index, basis, own, other, cotangent
    )
    parts = lax.all_to_all(partial, "graph", 0, 0)
    half = shape((pairs, 3 * share + SMALL_ROWS, width), BF16)
    dz_one, grads, other = call(
        tail_kernel,
        (shape((rows, width), BF16), half, half),
        core,
        parts,
        edge_feats,
        head,
        basis_grad,
        up_grad,
        early,
        early_other,
        scratch=[
            vmem((rows, width), BF16),
            vmem((rows, trip), BF16),
            vmem((width, width), BF16),
            vmem((owners, SMALL_ROWS, width), F32),
        ],
        smem=(0,),
        vmem=32,
    )
    other = swap(other)
    edge_grad = call(edge_kernel, shape((rows, width), BF16), dz_one, head, vmem=16)
    other, edge_grad = lax.optimization_barrier((other, edge_grad))
    chip = call(chip_sum_kernel, half, grads, other, vmem=16)
    chip = lax.all_to_all(chip, "dp", 0, 0, axis_index_groups=same_core)
    sums = call(
        owners_sum_kernel, shape((3 * share + SMALL_ROWS, width), BF16), chip, vmem=16
    )
    opposite = lax.ppermute(sums, "graph", [(peer, peer ^ 1) for peer in range(peers)])
    sums = call(
        pair_sum_kernel, shape((peers // 2,) + sums.shape, BF16), sums, opposite, vmem=16
    )
    along_y = [[2 * peer + side for peer in range(peers // 2)] for side in range(2)]
    sums = lax.all_to_all(sums, "graph", 0, 0, axis_index_groups=along_y)
    pair, down_grad, basis_grad, up, first, second = call(
        peers_sum_kernel,
        (
            shape((share, width), F32),
            shape((share, trip), F32),
            shape((1, trip), F32),
            shape((up_rows, width), F32),
            shape((share, width), F32),
            shape((share, width), F32),
        ),
        sums,
        vmem=16,
    )
    return edge_grad, pair, down_grad, basis_grad, up, first, second


def solution(mesh):
    split = P(("dp", "graph"), None)
    line = P(("dp", "graph"))
    rows = P("dp", None)
    return jax.shard_map(
        on_device,
        mesh=mesh,
        in_specs=(split, split, P(None, ("dp", "graph")), line, line) + (rows,) * 6,
        out_specs=(split,) + (rows,) * 6,
        check_vma=False,
    )
```
